32 devices in a mesh: dom: 8 (over z, x), mp: 4 (over y, core).
Axes of the slice: x: 2, y: 2, z: 4, core: 2. Of those that a mesh axis runs over, the one named last changes fastest.
Arguments:
- node_states: bfloat16 [2048, 1024], P(('dom', 'mp')), may hold values from -6 to 6
- edge_states: bfloat16 [6144, 1024], P(('dom', 'mp')), may hold values from -6 to 6
- edge_weight: bfloat16 [1024, 1024], P('mp'), may hold values from -0.109375 to 0.109375
- send_weight: bfloat16 [1024, 1024], P('mp'), may hold values from -0.109375 to 0.109375
- receive_weight: bfloat16 [1024, 1024], P('mp'), may hold values from -0.109375 to 0.109375
- output_weight: bfloat16 [1024, 1024], P('mp'), may hold values from -0.1875 to 0.1875
- norm_gain: float32 [1024], replicated, may hold values from 0.5 to 1.5
- senders: int32 [6144], P(('dom', 'mp')), may hold values from 0 to 127
- receivers: int32 [6144], P(('dom', 'mp')), may hold values from 0 to 63
- send_rows: int32 [32, 4, 16], P(('dom', 'mp')), may hold values from 0 to 63
- node_cotangent: bfloat16 [2048, 1024], P(('dom', 'mp')), may hold values from -6 to 6
- edge_cotangent: bfloat16 [6144, 1024], P(('dom', 'mp')), may hold values from -6 to 6
Outputs:
- new_nodes: bfloat16 [2048, 1024], P(('dom', 'mp'))
- new_edges: bfloat16 [6144, 1024], P(('dom', 'mp'))
- grad_nodes: bfloat16 [2048, 1024], P(('dom', 'mp'))
- grad_edges: bfloat16 [6144, 1024], P(('dom', 'mp'))
The draws below stay inside these ranges and needn't reach their ends.
Inputs may be any that keep to these rules, and one draw needn't show every extreme that they name: `senders`: A table row of the edge's own block. `receivers`: A node of the edge's own block. `send_rows`: local node indices of the sending block; a node may be listed more than once.
All inputs are finite; a program needn't handle non-finite values.
Results may differ from the reference program's by a relative error of at most 0.0059.
Values may be sent and summed in bfloat16 or wider, within the bound.
A program may use at most 64 MiB of HBM per device.

```python
import jax
import jax.numpy as jnp
from jax import lax

D = 1024
F = 1024
N_DEV = 64
SPAN = 2
HALO = 16
E_DEV = 192
TABLE = 128
BLOCKS = 32
NODES = 2048
EDGES = 6144


def touch_ends(array, own_key, smallest, top_value):
    spot = [jax.random.randint(jax.random.fold_in(own_key, axis), (), 0, length) for axis, length in enumerate(array.shape)]
    widest = array.shape.index(max(array.shape))
    next_to = spot[:widest] + [(spot[widest] + 1) % array.shape[widest]] + spot[widest + 1:]
    return array.at[tuple(spot)].set(smallest).at[tuple(next_to)].set(top_value)


def block_scale(rng, shape, split, low, largest):
    factor_of = 1.0
    for position, blocks in split:
        draws = jax.random.uniform(jax.random.fold_in(jax.random.fold_in(rng, 6), position), (blocks,), jnp.float32, low / len(split), largest / len(split))
        factor_of = factor_of * jnp.repeat(jnp.exp(draws), shape[position] // blocks).reshape((-1,) + (1,) * (len(shape) - 1 - position))
    return factor_of


def normal_values(rng, shape, scale, limit, cuts=(), kind=jnp.bfloat16):
    array = jax.random.normal(rng, shape, jnp.float32) * scale
    if len(cuts) > 0:
        array = block_scale(rng, shape, cuts, -0.22, 0.18) * array
    return jnp.clip(array, min=-limit, max=limit).astype(kind)


def setup_inputs(seed: int = 0) -> dict:
    key_of = jax.random.split(jax.random.key(seed), 13)
    node_states = normal_values(key_of[0], (NODES, D), 1.0, 6.0, ((0, 32),))
    edge_states = normal_values(key_of[1], (EDGES, D), 1.0, 6.0, ((0, 32),))
    edge_weight = normal_values(key_of[2], (D, F), (3 * D) ** -0.5, 0.109375, ((0, 4),))
    send_weight = normal_values(key_of[3], (D, F), (3 * D) ** -0.5, 0.109375, ((0, 4),))
    receive_weight = normal_values(key_of[4], (D, F), (3 * D) ** -0.5, 0.109375, ((0, 4),))
    output_weight = normal_values(key_of[5], (F, D), F ** -0.5, 0.1875, ((0, 4),))
    norm_gain = jnp.clip(1.0 + 0.1 * jax.random.normal(key_of[6], (D,), jnp.float32), 0.5, 1.5)
    senders = touch_ends(jax.random.randint(key_of[7], (EDGES,), 0, TABLE), jax.random.fold_in(key_of[7], 1), 0, TABLE - 1).astype(jnp.int32)
    receivers = touch_ends(jax.random.randint(key_of[8], (EDGES,), 0, N_DEV), jax.random.fold_in(key_of[8], 1), 0, N_DEV - 1).astype(jnp.int32)
    send_rows = touch_ends(jax.random.randint(key_of[9], (BLOCKS, 2 * SPAN, HALO), 0, N_DEV), jax.random.fold_in(key_of[9], 1), 0, N_DEV - 1).astype(jnp.int32)
    node_cotangent = normal_values(key_of[10], (NODES, D), 1.0, 6.0, ((0, 32),))
    edge_cotangent = normal_values(key_of[11], (EDGES, D), 1.0, 6.0, ((0, 32),))
    return dict(node_states=node_states, edge_states=edge_states, edge_weight=edge_weight, send_weight=send_weight, receive_weight=receive_weight, output_weight=output_weight, norm_gain=norm_gain, senders=senders, receivers=receivers, send_rows=send_rows, node_cotangent=node_cotangent, edge_cotangent=edge_cotangent)


eps = 1e-05

def normalize(values, norm_gain):
    average = lax.optimization_barrier(jnp.mean(values, axis=-1, keepdims=True))
    centred = values - average
    variance = lax.optimization_barrier(jnp.mean(centred * centred, axis=-1, keepdims=True))
    return centred * lax.rsqrt(variance + eps) * norm_gain.astype(jnp.float32)

def silu_slope(preact):
    sigmoid_value = jax.nn.sigmoid(preact)
    return sigmoid_value * (1.0 + preact * (1.0 - sigmoid_value))

def shift_list(spread):
    return [stride + 1 for stride in range(spread)] + [-(stride + 1) for stride in range(spread)]

def pick_rows(block_rows, row_ids):
    return jnp.take(block_rows, row_ids, axis=0)

def add_rows(totals, row_ids, values):
    return totals.at[row_ids].add(values)

def reference(node_states, edge_states, edge_weight, send_weight, receive_weight, output_weight, norm_gain, senders, receivers, send_rows, node_cotangent, edge_cotangent):
    blocks = node_states.shape[0] // N_DEV
    feature = node_states.shape[1]
    shifts = shift_list(SPAN)
    send_projection = jnp.dot(node_states, send_weight, preferred_element_type=jnp.float32).astype(jnp.bfloat16).reshape(blocks, N_DEV, F)
    receive_projection = jnp.dot(node_states, receive_weight, preferred_element_type=jnp.float32).astype(jnp.bfloat16).reshape(blocks, N_DEV, F)
    pieces = [send_projection]
    for block_index in range(2 * SPAN):
        chosen = jax.vmap(pick_rows)(send_projection, send_rows[:, block_index])
        pieces.append(jnp.roll(chosen, shifts[block_index], axis=0))
    lookup = jnp.concatenate(pieces, axis=1)

    def apply_norm(values):
        return normalize(values, norm_gain)

    def one_block(inputs):
        edge_block, lookup_block, receive_block, sender_ids, receiver_ids, node_block, node_grad, edge_grad = inputs
        preact = jnp.dot(edge_block, edge_weight, preferred_element_type=jnp.float32)
        preact = preact + jnp.take(lookup_block, sender_ids, axis=0).astype(jnp.float32)
        preact = preact + jnp.take(receive_block, receiver_ids, axis=0).astype(jnp.float32)
        hidden = jax.nn.silu(preact).astype(jnp.bfloat16)
        projected = jnp.dot(hidden, output_weight, preferred_element_type=jnp.float32)
        update, norm_back = jax.vjp(apply_norm, projected)
        new_edge = (edge_block.astype(jnp.float32) + update).astype(jnp.bfloat16)
        summed = jax.ops.segment_sum(new_edge.astype(jnp.float32), receiver_ids, num_segments=N_DEV)
        new_node = (node_block.astype(jnp.float32) + summed).astype(jnp.bfloat16)
        grad_total = edge_grad.astype(jnp.float32) + jnp.take(node_grad, receiver_ids, axis=0).astype(jnp.float32)
        grad_projected = norm_back(grad_total)[0].astype(jnp.bfloat16)
        grad_hidden = jnp.dot(grad_projected, output_weight.T, preferred_element_type=jnp.float32)
        grad_preact = (grad_hidden * silu_slope(preact)).astype(jnp.bfloat16)
        grad_edge = (grad_total + jnp.dot(grad_preact, edge_weight.T, preferred_element_type=jnp.float32)).astype(jnp.bfloat16)
        grad_lookup = jax.ops.segment_sum(grad_preact.astype(jnp.float32), sender_ids, num_segments=TABLE)
        grad_receive = jax.ops.segment_sum(grad_preact.astype(jnp.float32), receiver_ids, num_segments=N_DEV).astype(jnp.bfloat16)
        return (new_edge, new_node, grad_edge, grad_lookup[:N_DEV], grad_lookup[N_DEV:].astype(jnp.bfloat16), grad_receive)
    outputs = lax.map(one_block, (edge_states.reshape(blocks, E_DEV, feature), lookup, receive_projection, senders.reshape(blocks, E_DEV), receivers.reshape(blocks, E_DEV), node_states.reshape(blocks, N_DEV, feature), node_cotangent.reshape(blocks, N_DEV, feature), edge_cotangent.reshape(blocks, E_DEV, feature)))
    new_edges, new_nodes, grad_edges, own_grad, halo_grad, grad_receive = outputs
    halo_grad = halo_grad.reshape(blocks, 2 * SPAN, HALO, F)
    grad_send = own_grad
    for block_index in range(2 * SPAN):
        returned = jnp.roll(halo_grad[:, block_index], -shifts[block_index], axis=0).astype(jnp.float32)
        grad_send = jax.vmap(add_rows)(grad_send, send_rows[:, block_index], returned)
    grad_send = grad_send.astype(jnp.bfloat16).reshape(-1, F)
    grad_nodes = node_cotangent.astype(jnp.float32)
    grad_nodes = grad_nodes + jnp.dot(grad_send, send_weight.T, preferred_element_type=jnp.float32)
    grad_nodes = grad_nodes + jnp.dot(grad_receive.reshape(-1, F), receive_weight.T, preferred_element_type=jnp.float32)
    return (new_nodes.reshape(-1, feature), new_edges.reshape(-1, feature), grad_nodes.astype(jnp.bfloat16), grad_edges.reshape(-1, feature))
```

```python
import functools

import jax
import jax.numpy as jnp
from jax import lax
from jax.experimental import pallas as pl
from jax.experimental.pallas import tpu as pltpu
from jax.sharding import PartitionSpec as P

eps = 1e-05
MESH = pl.DeviceIdType.MESH
DIAGONAL = ((1, 1, 2), (1, 2, 1), (2, 1, 1), (2, 1, 1))


def product(left, right):
    return jnp.dot(left, right, preferred_element_type=jnp.float32)


def rows_product(left, right):
    return lax.dot_general(
        left, right, (((1,), (1,)), ((), ())), preferred_element_type=jnp.float32
    )


def kernel(
    doms, mps, square, shifts,
    node_h, edge_h, edge_w, send_w, receive_w, output_w, gain_h, send_h, receive_h, rows_h, node_g_h, edge_g_h,
    new_node_h, new_edge_h, grad_node_h, grad_edge_h,
    weights, node, edge, gain, sender, receiver, rows, node_g, edge_g,
    table, halo, back, returned, new_node, new_edge, grad_node, grad_edge,
    load_sem, store_sem, send_sem, recv_sem,
):
    dom, mp = lax.axis_index("dom"), lax.axis_index("mp")
    block = dom * mps + mp
    blocks = doms * mps
    count, halo_rows = node.shape[0], halo.shape[0] // len(shifts)
    panels = (send_w, receive_w, edge_w, output_w)
    size = send_w.shape[0]

    loads = []

    def load(source, target):
        copy = pltpu.make_async_copy(source, target, load_sem.at[len(loads)])
        copy.start()
        loads.append(copy)
        return copy

    own = pl.ds(pl.multiple_of(mp * size, size), size)
    load_panel = [load(panels[w], weights.at[w, own]) for w in range(4)]
    load_node = load(node_h, node)
    load_rows = load(rows_h, rows)
    load_sender = load(send_h, sender)
    load_receiver = load(receive_h, receiver)
    load_edge = load(edge_h, edge)
    load_gain = load(gain_h, gain)
    load_node_g = load(node_g_h, node_g)
    load_edge_g = load(edge_g_h, edge_g)

    def at_block(offset):
        other = lax.rem(block + offset + blocks, blocks)
        return (lax.div(other, mps), lax.rem(other, mps))

    if square:
        x, deep = lax.rem(dom, 2), lax.rem(lax.div(dom, 2), 2)
        core, y = lax.rem(mp, 2), lax.div(mp, 2)
        twin = (dom, mp + 1 - 2 * core)
        over_y = (dom, mp + 2 - 4 * y)
        over_x = (dom + 1 - 2 * x, mp)
        over_z = (dom + 2 - 4 * deep, mp)
        peers = [twin, over_y, over_x, over_z]
    else:
        peers = [(dom, lax.rem(mp + step, mps)) for step in range(1, mps)]
    barrier = pltpu.get_barrier_semaphore()
    greeted = peers + [at_block(shift) for shift in shifts]
    for peer in greeted:
        pl.semaphore_signal(barrier, inc=1, device_id=peer, device_id_type=MESH)
    pl.semaphore_wait(barrier, len(greeted))

    sent = []

    def send(source, target, peer):
        index = len(sent)
        copy = pltpu.make_async_remote_copy(
            src_ref=source, dst_ref=target, send_sem=send_sem.at[index], recv_sem=recv_sem.at[index],
            device_id=peer, device_id_type=MESH,
        )
        copy.start()
        sent.append(copy)
        return copy

    if square:
        unit = size // 16
        quarter = size // 4
        mine = x + 2 * deep
        by_x, by_z, opposite = mine + 1 - 2 * x, mine + 2 - 4 * deep, 3 - mine
        far = (mp + 2 - 4 * y) * size
        near = mp * size

        def part(w, base, start, length):
            return weights.at[w, pl.ds(pl.multiple_of(base + start, unit), length)]

        A, B, DY, X, Z, DX, DZ, SB, SX, SZ, SD = ([None] * 4 for _ in range(11))

        def begin_twin(w):
            A[w] = send(panels[w], weights.at[w, own], twin)

        def begin(w):
            B[w] = send(
                panels[w].at[pl.ds(pl.multiple_of(mine * quarter, quarter), quarter)],
                part(w, near, mine * quarter, quarter), over_y,
            )
            length = DIAGONAL[w][0] * unit
            DY[w] = send(
                panels[w].at[pl.ds(pl.multiple_of(opposite * quarter, quarter), length)],
                part(w, near, opposite * quarter, length), over_y,
            )

        def forward(w, start, length, peer):
            region = part(w, far, start, length)
            return send(region, region, peer)

        def step1(w):
            B[w].wait_recv()
            X[w] = forward(w, mine * quarter, quarter, over_x)
            Z[w] = forward(w, mine * quarter, quarter, over_z)
            SB[w] = forward(w, mine * quarter, quarter, twin)

        def step2(w):
            dy, dx, dz = (units * unit for units in DIAGONAL[w])
            X[w].wait_recv()
            DZ[w] = forward(w, by_x * quarter + dy + dx, dz, over_z)
            SX[w] = forward(w, by_x * quarter, quarter, twin)
            Z[w].wait_recv()
            DX[w] = forward(w, by_z * quarter + dy, dx, over_x)
            SZ[w] = forward(w, by_z * quarter, quarter, twin)

        def step3(w):
            DY[w].wait_recv()
            DX[w].wait_recv()
            DZ[w].wait_recv()
            SD[w] = forward(w, opposite * quarter, quarter, twin)

        def step4(w):
            load_panel[w].wait()
            for copy in (A[w], SB[w], SX[w], SZ[w], SD[w]):
                copy.wait_recv()
    else:
        direct = [[send(panels[w], weights.at[w, own], peer) for peer in peers] for w in range(4)]

        def step4(w):
            load_panel[w].wait()
            for copy in direct[w]:
                copy.wait_recv()

    def project_send():
        load_node.wait()
        load_rows.wait()
        table[:count] = product(node[...], weights[0]).astype(jnp.bfloat16)
        pick = (lax.broadcasted_iota(jnp.int32, (count, halo.shape[0]), 0) == rows[...]).astype(jnp.float32)
        halo[...] = product(pick.T.astype(jnp.bfloat16), table[:count]).astype(jnp.bfloat16)
        arrive = []
        for j, shift in enumerate(shifts):
            arrive.append(send(
                halo.at[pl.ds(j * halo_rows, halo_rows)],
                table.at[pl.ds(count + j * halo_rows, halo_rows)], at_block(shift),
            ))
        return pick.astype(jnp.bfloat16), arrive

    lookup_rows = count + halo.shape[0]

    def project_receive():
        table[lookup_rows:] = product(node[...], weights[1]).astype(jnp.bfloat16)

    if square:
        for w in range(4):
            begin_twin(w)
        begin(0)
        begin(1)
        step1(0)
        begin(2)
        step2(0)
        step1(1)
        begin(3)
        step3(0)
        step2(1)
        step4(0)
        pick, arrive = project_send()
        step1(2)
        step3(1)
        step2(2)
        step4(1)
        project_receive()
        step1(3)
        step3(2)
        step2(3)
        step4(2)
    else:
        step4(0)
        pick, arrive = project_send()
        step4(1)
        project_receive()
        step4(2)

    for copy in (load_edge, load_sender, load_receiver, load_gain, load_node_g, load_edge_g):
        copy.wait()
    edges = edge.shape[0]
    by_sender = lax.broadcasted_iota(jnp.int32, (lookup_rows, edges), 0) == sender[...]
    by_receiver = lax.broadcasted_iota(jnp.int32, (count, edges), 0) == receiver[...]
    to_table = jnp.concatenate([by_sender.astype(jnp.float32), by_receiver.astype(jnp.float32)], axis=0)
    from_table = to_table.T.astype(jnp.bfloat16)
    to_receiver = by_receiver.astype(jnp.float32)
    from_receiver = to_receiver.T.astype(jnp.bfloat16)
    to_table = to_table.astype(jnp.bfloat16)
    to_receiver = to_receiver.astype(jnp.bfloat16)

    preact = product(edge[...], weights[2])
    if square:
        step3(3)
    grad_total = edge_g[...].astype(jnp.float32) + product(from_receiver, node_g[...])
    for copy in arrive:
        copy.wait_recv()
    preact = preact + product(from_table, table[...])
    sigmoid = jax.nn.sigmoid(preact)
    hidden = (preact * sigmoid).astype(jnp.bfloat16)
    slope = sigmoid * (1.0 + preact * (1.0 - sigmoid))
    scaled = grad_total * gain[...]

    step4(3)
    projected = product(hidden, weights[3])
    centred = projected - jnp.mean(projected, axis=-1, keepdims=True)
    variance = jnp.mean(centred * centred, axis=-1, keepdims=True)
    scale = lax.rsqrt(variance + eps)
    unit_rows = centred * scale
    new_edge[...] = (edge[...].astype(jnp.float32) + unit_rows * gain[...]).astype(jnp.bfloat16)

    stores = []

    def store(source, target):
        copy = pltpu.make_async_copy(source, target, store_sem.at[len(stores)])
        copy.start()
        stores.append(copy)

    store(new_edge, new_edge_h)
    along = jnp.mean(scaled * unit_rows, axis=-1, keepdims=True)
    grad_projected = scale * (scaled - jnp.mean(scaled, axis=-1, keepdims=True) - unit_rows * along)
    grad_hidden = rows_product(grad_projected.astype(jnp.bfloat16), weights[3])
    grad_preact = (grad_hidden * slope).astype(jnp.bfloat16)
    grad_table = product(to_table, grad_preact)
    back[...] = grad_table[count:lookup_rows].astype(jnp.bfloat16)
    home = []
    for j, shift in enumerate(shifts):
        piece = pl.ds(j * halo_rows, halo_rows)
        home.append(send(back.at[piece], returned.at[piece], at_block(-shift)))
    grad_edge[...] = (grad_total + rows_product(grad_preact, weights[2])).astype(jnp.bfloat16)
    store(grad_edge, grad_edge_h)
    new_node[...] = (node[...].astype(jnp.float32) + product(to_receiver, new_edge[...])).astype(jnp.bfloat16)
    store(new_node, new_node_h)
    grad_nodes = node_g[...].astype(jnp.float32) + rows_product(
        grad_table[lookup_rows:].astype(jnp.bfloat16), weights[1]
    )
    for copy in home:
        copy.wait_recv()
    grad_send = (grad_table[:count] + product(pick, returned[...])).astype(jnp.bfloat16)
    grad_node[...] = (grad_nodes + rows_product(grad_send, weights[0])).astype(jnp.bfloat16)
    store(grad_node, grad_node_h)
    for copy in sent:
        copy.wait_send()
    for copy in stores:
        copy.wait()


def solution(mesh):
    doms, mps = mesh.shape["dom"], mesh.shape["mp"]

    def shards(
        node_states, edge_states, edge_weight, send_weight, receive_weight, output_weight,
        norm_gain, senders, receivers, send_rows, node_cotangent, edge_cotangent,
    ):
        nodes, width = node_states.shape
        edges = edge_states.shape[0]
        hidden = edge_weight.shape[1]
        spread, halo_rows = send_rows.shape[1] // 2, send_rows.shape[2]
        halos = 2 * spread * halo_rows
        shifts = [step + 1 for step in range(spread)] + [-(step + 1) for step in range(spread)]
        square = mps == 4 and doms % 4 == 0 and edge_weight.shape[0] % 256 == 0
        copies = 4 * (13 if square else mps - 1) + 4 * spread
        any_space = pl.BlockSpec(memory_space=pl.ANY)
        bf16 = jnp.bfloat16
        return pl.pallas_call(
            functools.partial(kernel, doms, mps, square, shifts),
            out_shape=(
                jax.ShapeDtypeStruct((nodes, width), bf16),
                jax.ShapeDtypeStruct((edges, width), bf16),
                jax.ShapeDtypeStruct((nodes, width), bf16),
                jax.ShapeDtypeStruct((edges, width), bf16),
            ),
            in_specs=[any_space] * 12,
            out_specs=(any_space,) * 4,
            scratch_shapes=[
                pltpu.VMEM((4, width, hidden), bf16),
                pltpu.VMEM((nodes, width), bf16),
                pltpu.VMEM((edges, width), bf16),
                pltpu.VMEM((1, width), jnp.float32),
                pltpu.VMEM((1, edges), jnp.int32),
                pltpu.VMEM((1, edges), jnp.int32),
                pltpu.VMEM((1, halos), jnp.int32),
                pltpu.VMEM((nodes, width), bf16),
                pltpu.VMEM((edges, width), bf16),
                pltpu.VMEM((2 * nodes + halos, hidden), bf16),
                pltpu.VMEM((halos, hidden), bf16),
                pltpu.VMEM((halos, hidden), bf16),
                pltpu.VMEM((halos, hidden), bf16),
                pltpu.VMEM((nodes, width), bf16),
                pltpu.VMEM((edges, width), bf16),
                pltpu.VMEM((nodes, width), bf16),
                pltpu.VMEM((edges, width), bf16),
                pltpu.SemaphoreType.DMA((12,)),
                pltpu.SemaphoreType.DMA((4,)),
                pltpu.SemaphoreType.DMA((copies,)),
                pltpu.SemaphoreType.DMA((copies,)),
            ],
            compiler_params=pltpu.CompilerParams(
                collective_id=0, has_side_effects=True, vmem_limit_bytes=60 * 1024 * 1024
            ),
            cost_estimate=pl.CostEstimate(flops=2 * width * hidden * 4 * (nodes + edges), bytes_accessed=16 * width * hidden, transcendentals=edges * hidden),
        )(
            node_states, edge_states, edge_weight, send_weight, receive_weight, output_weight,
            norm_gain.reshape(1, width), senders.reshape(1, edges), receivers.reshape(1, edges),
            send_rows.reshape(1, halos), node_cotangent, edge_cotangent,
        )

    rows = P(("dom", "mp"), None)
    panel = P("mp", None)
    indices = P(("dom", "mp"))
    return jax.shard_map(
        shards,
        mesh=mesh,
        in_specs=(rows, rows, panel, panel, panel, panel, P(), indices, indices, P(("dom", "mp"), None, None), rows, rows),
        out_specs=(rows,) * 4,
        check_vma=False,
    )
```

```python
import functools

import jax
import jax.numpy as jnp
from jax import lax
from jax.experimental import pallas as pl
from jax.experimental.pallas import tpu as pltpu
from jax.sharding import PartitionSpec as P

eps = 1e-05
MESH = pl.DeviceIdType.MESH
DIAGONAL = ((1, 1, 2), (1, 2, 1), (2, 1, 1), (2, 1, 1))


def product(left, right):
    return jnp.dot(left, right, preferred_element_type=jnp.float32)


def rows_product(left, right):
    return lax.dot_general(
        left, right, (((1,), (1,)), ((), ())), preferred_element_type=jnp.float32
    )


def kernel(
    doms, mps, square, shifts,
    node_h, edge_h, edge_w, send_w, receive_w, output_w, gain_h, send_h, receive_h, rows_h, node_g_h, edge_g_h,
    new_node_h, new_edge_h, grad_node_h, grad_edge_h,
    weights, node, edge, gain, sender, receiver, rows, node_g, edge_g,
    table, halo, back, returned, new_node, new_edge, grad_node, grad_edge,
    wide, slope, grad_total, scaled, hidden, grad_projected, grad_preact,
    load_sem, store_sem, send_sem, recv_sem,
):
    dom, mp = lax.axis_index("dom"), lax.axis_index("mp")
    block = dom * mps + mp
    blocks = doms * mps
    count, halo_rows = node.shape[0], halo.shape[0] // len(shifts)
    panels = (send_w, receive_w, edge_w, output_w)
    size = send_w.shape[0]

    loads = []

    def load(source, target):
        copy = pltpu.make_async_copy(source, target, load_sem.at[len(loads)])
        copy.start()
        loads.append(copy)
        return copy

    own = pl.ds(pl.multiple_of(mp * size, size), size)
    load_panel = [load(panels[w], weights.at[w, own]) for w in range(4)]
    load_node = load(node_h, node)
    load_rows = load(rows_h, rows)
    load_sender = load(send_h, sender)
    load_receiver = load(receive_h, receiver)
    load_edge = load(edge_h, edge)
    load_gain = load(gain_h, gain)
    load_node_g = load(node_g_h, node_g)
    load_edge_g = load(edge_g_h, edge_g)

    def at_block(offset):
        other = lax.rem(block + offset + blocks, blocks)
        return (lax.div(other, mps), lax.rem(other, mps))

    if square:
        x, deep = lax.rem(dom, 2), lax.rem(lax.div(dom, 2), 2)
        core, y = lax.rem(mp, 2), lax.div(mp, 2)
        twin = (dom, mp + 1 - 2 * core)
        over_y = (dom, mp + 2 - 4 * y)
        over_x = (dom + 1 - 2 * x, mp)
        over_z = (dom + 2 - 4 * deep, mp)
        peers = [twin, over_y, over_x, over_z]
    else:
        peers = [(dom, lax.rem(mp + step, mps)) for step in range(1, mps)]
    barrier = pltpu.get_barrier_semaphore()
    greeted = peers + [at_block(shift) for shift in shifts]
    for peer in greeted:
        pl.semaphore_signal(barrier, inc=1, device_id=peer, device_id_type=MESH)
    pl.semaphore_wait(barrier, len(greeted))

    sent = []

    def send(source, target, peer):
        index = len(sent)
        copy = pltpu.make_async_remote_copy(
            src_ref=source, dst_ref=target, send_sem=send_sem.at[index], recv_sem=recv_sem.at[index],
            device_id=peer, device_id_type=MESH,
        )
        copy.start()
        sent.append(copy)
        return copy

    if square:
        unit = size // 16
        quarter = size // 4
        mine = x + 2 * deep
        by_x, by_z, opposite = mine + 1 - 2 * x, mine + 2 - 4 * deep, 3 - mine
        far = (mp + 2 - 4 * y) * size
        near = mp * size

        def part(w, base, start, length):
            return weights.at[w, pl.ds(pl.multiple_of(base + start, unit), length)]

        A, B, DY, X, Z, DX, DZ, SB, SX, SZ, SD = ([None] * 4 for _ in range(11))

        def begin_twin(w):
            A[w] = send(panels[w], weights.at[w, own], twin)

        def begin(w):
            B[w] = send(
                panels[w].at[pl.ds(pl.multiple_of(mine * quarter, quarter), quarter)],
                part(w, near, mine * quarter, quarter), over_y,
            )

        def begin_diagonal(w):
            length = DIAGONAL[w][0] * unit
            DY[w] = send(
                panels[w].at[pl.ds(pl.multiple_of(opposite * quarter, quarter), length)],
                part(w, near, opposite * quarter, length), over_y,
            )

        def forward(w, start, length, peer):
            region = part(w, far, start, length)
            return send(region, region, peer)

        def step1(w):
            B[w].wait_recv()
            X[w] = forward(w, mine * quarter, quarter, over_x)
            Z[w] = forward(w, mine * quarter, quarter, over_z)
            if w < 2:
                begin(w + 2)
                begin_diagonal(w)
            elif w == 2:
                begin_diagonal(2)
                begin_diagonal(3)
            SB[w] = forward(w, mine * quarter, quarter, twin)

        def step2(w):
            dy, dx, dz = (units * unit for units in DIAGONAL[w])
            X[w].wait_recv()
            DZ[w] = forward(w, by_x * quarter + dy + dx, dz, over_z)
            SX[w] = forward(w, by_x * quarter, quarter, twin)
            Z[w].wait_recv()
            DX[w] = forward(w, by_z * quarter + dy, dx, over_x)
            SZ[w] = forward(w, by_z * quarter, quarter, twin)

        def step3(w):
            DY[w].wait_recv()
            DX[w].wait_recv()
            DZ[w].wait_recv()
            SD[w] = forward(w, opposite * quarter, quarter, twin)

        def step4(w):
            load_panel[w].wait()
            for copy in (A[w], SB[w], SX[w], SZ[w], SD[w]):
                copy.wait_recv()
    else:
        direct = [[send(panels[w], weights.at[w, own], peer) for peer in peers] for w in range(4)]

        def step4(w):
            load_panel[w].wait()
            for copy in direct[w]:
                copy.wait_recv()

    def project_send():
        load_node.wait()
        load_rows.wait()
        chosen = jnp.concatenate([rows[0, j : j + 1, :] for j in range(len(shifts))], axis=1)
        table[:count] = product(node[...], weights[0]).astype(jnp.bfloat16)
        pick = (lax.broadcasted_iota(jnp.int32, (count, halo.shape[0]), 0) == chosen).astype(jnp.float32)
        halo[...] = product(pick.T.astype(jnp.bfloat16), table[:count]).astype(jnp.bfloat16)
        arrive = []
        for j, shift in enumerate(shifts):
            arrive.append(send(
                halo.at[pl.ds(j * halo_rows, halo_rows)],
                table.at[pl.ds(count + j * halo_rows, halo_rows)], at_block(shift),
            ))
        return pick.astype(jnp.bfloat16), arrive

    lookup_rows = count + halo.shape[0]

    def project_receive():
        table[lookup_rows:] = product(node[...], weights[1]).astype(jnp.bfloat16)

    if square:
        begin(0)
        begin(1)
        begin_twin(0)
        begin_twin(1)
        step1(0)
        begin_twin(2)
        step1(1)
        begin_twin(3)
        step2(0)
        step1(2)
        step2(1)
        step3(0)
        step1(3)
        step2(2)
        step3(1)
        step4(0)
        pick, arrive = project_send()
        step2(3)
        step3(2)
        step4(1)
        project_receive()
        step3(3)
        step4(2)
    else:
        step4(0)
        pick, arrive = project_send()
        step4(1)
        project_receive()
        step4(2)

    for copy in (load_edge, load_sender, load_receiver, load_gain, load_node_g, load_edge_g):
        copy.wait()
    edges = edge.shape[0]
    by_sender = lax.broadcasted_iota(jnp.int32, (lookup_rows, edges), 0) == sender[...]
    by_receiver = lax.broadcasted_iota(jnp.int32, (count, edges), 0) == receiver[...]
    to_table = jnp.concatenate([by_sender.astype(jnp.float32), by_receiver.astype(jnp.float32)], axis=0)
    from_table = to_table.T.astype(jnp.bfloat16)
    to_receiver = by_receiver.astype(jnp.float32)
    from_receiver = to_receiver.T.astype(jnp.bfloat16)
    to_table = to_table.astype(jnp.bfloat16)
    to_receiver = to_receiver.astype(jnp.bfloat16)

    strips = [pl.ds(start, 16) for start in range(0, edges, 16)]
    grad_total[...] = edge_g[...].astype(jnp.float32) + product(from_receiver, node_g[...])
    for strip in strips:
        values = grad_total[strip] * gain[...]
        scaled[strip] = values - jnp.mean(values, axis=-1, keepdims=True)
    wide[...] = product(edge[...], weights[2])
    for copy in arrive:
        copy.wait_recv()
    wide[...] += product(from_table, table[...])
    for strip in strips:
        values = wide[strip]
        sigmoid = jax.nn.sigmoid(values)
        hidden[strip] = (values * sigmoid).astype(jnp.bfloat16)
        slope[strip] = sigmoid * (1.0 + values * (1.0 - sigmoid))

    step4(3)
    wide[...] = product(hidden[...], weights[3])
    for strip in strips:
        values = wide[strip]
        centred = values - jnp.mean(values, axis=-1, keepdims=True)
        variance = jnp.mean(centred * centred, axis=-1, keepdims=True)
        along = jnp.mean(scaled[strip] * centred, axis=-1, keepdims=True)
        scale = lax.rsqrt(variance + eps)
        unit_rows = centred * scale
        new_edge[strip] = (edge[strip].astype(jnp.float32) + unit_rows * gain[...]).astype(jnp.bfloat16)
        grad_projected[strip] = (scale * (scaled[strip] - unit_rows * (scale * along))).astype(jnp.bfloat16)

    stores = []

    def store(source, target):
        copy = pltpu.make_async_copy(source, target, store_sem.at[len(stores)])
        copy.start()
        stores.append(copy)

    store(new_edge, new_edge_h)
    wide[...] = rows_product(grad_projected[...], weights[3])
    for strip in strips:
        grad_preact[strip] = (wide[strip] * slope[strip]).astype(jnp.bfloat16)
    grad_table = product(to_table, grad_preact[...])
    back[...] = grad_table[count:lookup_rows].astype(jnp.bfloat16)
    home = []
    for j, shift in enumerate(shifts):
        piece = pl.ds(j * halo_rows, halo_rows)
        home.append(send(back.at[piece], returned.at[piece], at_block(-shift)))
    grad_edge[...] = (grad_total[...] + rows_product(grad_preact[...], weights[2])).astype(jnp.bfloat16)
    store(grad_edge, grad_edge_h)
    new_node[...] = (node[...].astype(jnp.float32) + product(to_receiver, new_edge[...])).astype(jnp.bfloat16)
    store(new_node, new_node_h)
    grad_nodes = node_g[...].astype(jnp.float32) + rows_product(
        grad_table[lookup_rows:].astype(jnp.bfloat16), weights[1]
    )
    for copy in home:
        copy.wait_recv()
    grad_send = (grad_table[:count] + product(pick, returned[...])).astype(jnp.bfloat16)
    grad_node[...] = (grad_nodes + rows_product(grad_send, weights[0])).astype(jnp.bfloat16)
    store(grad_node, grad_node_h)
    for copy in sent:
        copy.wait_send()
    for copy in stores:
        copy.wait()


def hand_out(*refs):
    copies = [pltpu.make_async_copy(refs[i], refs[4 + i], refs[8].at[i]) for i in range(4)]
    for copy in copies:
        copy.start()
    for copy in copies:
        copy.wait()


def solution(mesh):
    doms, mps = mesh.shape["dom"], mesh.shape["mp"]

    def shards(
        node_states, edge_states, edge_weight, send_weight, receive_weight, output_weight,
        norm_gain, senders, receivers, send_rows, node_cotangent, edge_cotangent,
    ):
        nodes, width = node_states.shape
        edges = edge_states.shape[0]
        hidden = edge_weight.shape[1]
        spread, halo_rows = send_rows.shape[1] // 2, send_rows.shape[2]
        halos = 2 * spread * halo_rows
        shifts = [step + 1 for step in range(spread)] + [-(step + 1) for step in range(spread)]
        square = mps == 4 and doms % 4 == 0 and edge_weight.shape[0] % 256 == 0
        copies = 4 * (13 if square else mps - 1) + 4 * spread
        any_space = pl.BlockSpec(memory_space=pl.ANY)
        bf16 = jnp.bfloat16
        results = pl.pallas_call(
            functools.partial(kernel, doms, mps, square, shifts),
            out_shape=(
                jax.ShapeDtypeStruct((nodes, width), bf16),
                jax.ShapeDtypeStruct((edges, width), bf16),
                jax.ShapeDtypeStruct((nodes, width), bf16),
                jax.ShapeDtypeStruct((edges, width), bf16),
            ),
            in_specs=[pl.BlockSpec(memory_space=pltpu.HBM)] * 12,
            out_specs=(any_space,) * 4,
            scratch_shapes=[
                pltpu.VMEM((4, width, hidden), bf16),
                pltpu.VMEM((nodes, width), bf16),
                pltpu.VMEM((edges, width), bf16),
                pltpu.VMEM((1, width), jnp.float32),
                pltpu.VMEM((1, edges), jnp.int32),
                pltpu.VMEM((1, edges), jnp.int32),
                pltpu.VMEM(send_rows.shape, jnp.int32),
                pltpu.VMEM((nodes, width), bf16),
                pltpu.VMEM((edges, width), bf16),
                pltpu.VMEM((2 * nodes + halos, hidden), bf16),
                pltpu.VMEM((halos, hidden), bf16),
                pltpu.VMEM((halos, hidden), bf16),
                pltpu.VMEM((halos, hidden), bf16),
                pltpu.VMEM((nodes, width), bf16),
                pltpu.VMEM((edges, width), bf16),
                pltpu.VMEM((nodes, width), bf16),
                pltpu.VMEM((edges, width), bf16),
                pltpu.VMEM((edges, hidden), jnp.float32),
                pltpu.VMEM((edges, hidden), jnp.float32),
                pltpu.VMEM((edges, width), jnp.float32),
                pltpu.VMEM((edges, width), jnp.float32),
                pltpu.VMEM((edges, hidden), bf16),
                pltpu.VMEM((edges, width), bf16),
                pltpu.VMEM((edges, hidden), bf16),
                pltpu.SemaphoreType.DMA((12,)),
                pltpu.SemaphoreType.DMA((4,)),
                pltpu.SemaphoreType.DMA((copies,)),
                pltpu.SemaphoreType.DMA((copies,)),
            ],
            compiler_params=pltpu.CompilerParams(
                collective_id=0, has_side_effects=True, vmem_limit_bytes=60 * 1024 * 1024
            ),
            cost_estimate=pl.CostEstimate(flops=2 * width * hidden * 4 * (nodes + edges), bytes_accessed=16 * width * hidden, transcendentals=edges * hidden),
        )(
            node_states, edge_states, edge_weight, send_weight, receive_weight, output_weight,
            norm_gain.reshape(1, width), senders.reshape(1, edges), receivers.reshape(1, edges),
            send_rows, node_cotangent, edge_cotangent,
        )
        return pl.pallas_call(
            hand_out,
            out_shape=tuple(jax.ShapeDtypeStruct(result.shape, bf16) for result in results),
            in_specs=[any_space] * 4,
            out_specs=(any_space,) * 4,
            scratch_shapes=[pltpu.SemaphoreType.DMA((4,))],
        )(*results)

    rows = P(("dom", "mp"), None)
    panel = P("mp", None)
    indices = P(("dom", "mp"))
    return jax.shard_map(
        shards,
        mesh=mesh,
        in_specs=(rows, rows, panel, panel, panel, panel, P(), indices, indices, P(("dom", "mp"), None, None), rows, rows),
        out_specs=(rows,) * 4,
        check_vma=False,
    )
```

```python
import functools

import jax
import jax.numpy as jnp
from jax import lax
from jax.experimental import pallas as pl
from jax.experimental.pallas import tpu as pltpu
from jax.sharding import PartitionSpec as P

eps = 1e-05
MESH = pl.DeviceIdType.MESH
DIAGONAL = ((0, 2, 2), (0, 2, 2), (4, 0, 0), (4, 0, 0))


def product(left, right):
    return jnp.dot(left, right, preferred_element_type=jnp.float32)


def rows_product(left, right):
    return lax.dot_general(
        left, right, (((1,), (1,)), ((), ())), preferred_element_type=jnp.float32
    )


def kernel(
    doms, mps, square, shifts,
    node_h, edge_h, edge_w, send_w, receive_w, output_w, gain_h, send_h, receive_h, rows_h, node_g_h, edge_g_h,
    new_node, new_edge, grad_node, grad_edge,
    weights, node, edge, gain, sender, receiver, rows, node_g, edge_g,
    table, halo, back, returned,
    wide, slope, grad_total, scaled, hidden, grad_projected, grad_preact,
    load_sem, send_sem, recv_sem,
):
    dom, mp = lax.axis_index("dom"), lax.axis_index("mp")
    block = dom * mps + mp
    blocks = doms * mps
    count, halo_rows = node.shape[0], halo.shape[0] // len(shifts)
    panels = (send_w, edge_w, receive_w, output_w)
    size = send_w.shape[0]

    loads = []

    def load(source, target):
        copy = pltpu.make_async_copy(source, target, load_sem.at[len(loads)])
        copy.start()
        loads.append(copy)
        return copy

    own = pl.ds(pl.multiple_of(mp * size, size), size)
    load_panel = [load(panels[w], weights.at[w, own]) for w in range(4)]
    load_node = load(node_h, node)
    load_rows = load(rows_h, rows)
    load_sender = load(send_h, sender)
    load_receiver = load(receive_h, receiver)
    load_edge = load(edge_h, edge)
    load_gain = load(gain_h, gain)
    load_node_g = load(node_g_h, node_g)
    load_edge_g = load(edge_g_h, edge_g)

    def at_block(offset):
        other = lax.rem(block + offset + blocks, blocks)
        return (lax.div(other, mps), lax.rem(other, mps))

    if square:
        x, deep = lax.rem(dom, 2), lax.rem(lax.div(dom, 2), 2)
        core, y = lax.rem(mp, 2), lax.div(mp, 2)
        twin = (dom, mp + 1 - 2 * core)
        over_y = (dom, mp + 2 - 4 * y)
        over_x = (dom + 1 - 2 * x, mp)
        over_z = (dom + 2 - 4 * deep, mp)
        peers = [twin, over_y, over_x, over_z]
    else:
        peers = [(dom, lax.rem(mp + step, mps)) for step in range(1, mps)]
    barrier = pltpu.get_barrier_semaphore()
    greeted = peers + [at_block(shift) for shift in shifts]
    for peer in greeted:
        pl.semaphore_signal(barrier, inc=1, device_id=peer, device_id_type=MESH)
    pl.semaphore_wait(barrier, len(greeted))

    sent = []

    def send(source, target, peer):
        index = len(sent)
        copy = pltpu.make_async_remote_copy(
            src_ref=source, dst_ref=target, send_sem=send_sem.at[index], recv_sem=recv_sem.at[index],
            device_id=peer, device_id_type=MESH,
        )
        copy.start()
        sent.append(copy)
        return copy

    if square:
        unit = size // 16
        quarter = size // 4
        mine = x + 2 * deep
        by_x, by_z, opposite = mine + 1 - 2 * x, mine + 2 - 4 * deep, 3 - mine
        far = (mp + 2 - 4 * y) * size
        near = mp * size

        def part(w, base, start, length):
            return weights.at[w, pl.ds(pl.multiple_of(base + start, unit), length)]

        A, B, DY, X, Z, DX, DZ, SB, SX, SZ, SD = ([None] * 4 for _ in range(11))

        def begin_twin(w):
            A[w] = send(panels[w], weights.at[w, own], twin)

        def begin(w):
            B[w] = send(
                panels[w].at[pl.ds(pl.multiple_of(mine * quarter, quarter), quarter)],
                part(w, near, mine * quarter, quarter), over_y,
            )

        def begin_diagonal(w):
            length = DIAGONAL[w][0] * unit
            DY[w] = send(
                panels[w].at[pl.ds(pl.multiple_of(opposite * quarter, quarter), length)],
                part(w, near, opposite * quarter, length), over_y,
            )

        def forward(w, start, length, peer):
            region = part(w, far, start, length)
            return send(region, region, peer)

        def step1(w):
            B[w].wait_recv()
            X[w] = forward(w, mine * quarter, quarter, over_x)
            Z[w] = forward(w, mine * quarter, quarter, over_z)
            if w == 0:
                begin(2)
            elif w == 1:
                begin(3)
            else:
                begin_diagonal(w)
            SB[w] = forward(w, mine * quarter, quarter, twin)

        def step2(w):
            dy, dx, dz = (units * unit for units in DIAGONAL[w])
            X[w].wait_recv()
            if dz:
                DZ[w] = forward(w, by_x * quarter + dy + dx, dz, over_z)
            SX[w] = forward(w, by_x * quarter, quarter, twin)
            Z[w].wait_recv()
            if dx:
                DX[w] = forward(w, by_z * quarter + dy, dx, over_x)
            SZ[w] = forward(w, by_z * quarter, quarter, twin)

        def step3(w):
            for copy in (DY[w], DX[w], DZ[w]):
                if copy is not None:
                    copy.wait_recv()
            SD[w] = forward(w, opposite * quarter, quarter, twin)

        def step4(w):
            load_panel[w].wait()
            for copy in (A[w], SB[w], SX[w], SZ[w], SD[w]):
                copy.wait_recv()
    else:
        direct = [[send(panels[w], weights.at[w, own], peer) for peer in peers] for w in range(4)]

        def step4(w):
            load_panel[w].wait()
            for copy in direct[w]:
                copy.wait_recv()

    def project_send():
        load_node.wait()
        load_rows.wait()
        chosen = jnp.concatenate([rows[0, j : j + 1, :] for j in range(len(shifts))], axis=1)
        table[:count] = product(node[...], weights[0]).astype(jnp.bfloat16)
        pick = (lax.broadcasted_iota(jnp.int32, (count, halo.shape[0]), 0) == chosen).astype(jnp.float32)
        halo[...] = product(pick.T.astype(jnp.bfloat16), table[:count]).astype(jnp.bfloat16)
        arrive = []
        for j, shift in enumerate(shifts):
            arrive.append(send(
                halo.at[pl.ds(j * halo_rows, halo_rows)],
                table.at[pl.ds(count + j * halo_rows, halo_rows)], at_block(shift),
            ))
        return pick.astype(jnp.bfloat16), arrive

    lookup_rows = count + halo.shape[0]

    def project_receive():
        table[lookup_rows:] = product(node[...], weights[2]).astype(jnp.bfloat16)

    if square:
        begin(0)
        begin(1)
        begin_twin(0)
        begin_twin(1)
    for copy in (load_edge, load_sender, load_receiver, load_gain, load_node_g, load_edge_g):
        copy.wait()
    edges = edge.shape[0]
    by_sender = lax.broadcasted_iota(jnp.int32, (lookup_rows, edges), 0) == sender[...]
    by_receiver = lax.broadcasted_iota(jnp.int32, (count, edges), 0) == receiver[...]
    to_table = jnp.concatenate([by_sender.astype(jnp.float32), by_receiver.astype(jnp.float32)], axis=0)
    from_table = to_table.T.astype(jnp.bfloat16)
    to_receiver = by_receiver.astype(jnp.float32)
    from_receiver = to_receiver.T.astype(jnp.bfloat16)
    to_table = to_table.astype(jnp.bfloat16)
    to_receiver = to_receiver.astype(jnp.bfloat16)

    strips = [pl.ds(start, 16) for start in range(0, edges, 16)]
    grad_total[...] = edge_g[...].astype(jnp.float32) + product(from_receiver, node_g[...])
    for strip in strips:
        values = grad_total[strip] * gain[...]
        scaled[strip] = values - jnp.mean(values, axis=-1, keepdims=True)
    if square:
        step1(0)
        begin_twin(2)
        step1(1)
        begin_twin(3)
        step2(0)
        step1(2)
        step2(1)
        step3(0)
        step1(3)
        step4(0)
        pick, arrive = project_send()
        step2(2)
        step3(1)
        step4(1)
        wide[...] = product(edge[...], weights[1])
        step3(2)
        step2(3)
        step3(3)
        step4(2)
    else:
        step4(0)
        pick, arrive = project_send()
        step4(1)
        wide[...] = product(edge[...], weights[1])
        step4(2)
    project_receive()

    for copy in arrive:
        copy.wait_recv()
    wide[...] += product(from_table, table[...])
    for strip in strips:
        values = wide[strip]
        sigmoid = jax.nn.sigmoid(values)
        hidden[strip] = (values * sigmoid).astype(jnp.bfloat16)
        slope[strip] = sigmoid * (1.0 + values * (1.0 - sigmoid))

    step4(3)
    wide[...] = product(hidden[...], weights[3])
    for strip in strips:
        values = wide[strip]
        centred = values - jnp.mean(values, axis=-1, keepdims=True)
        variance = jnp.mean(centred * centred, axis=-1, keepdims=True)
        along = jnp.mean(scaled[strip] * centred, axis=-1, keepdims=True)
        scale = lax.rsqrt(variance + eps)
        unit_rows = centred * scale
        new_edge[strip] = (edge[strip].astype(jnp.float32) + unit_rows * gain[...]).astype(jnp.bfloat16)
        grad_projected[strip] = (scale * (scaled[strip] - unit_rows * (scale * along))).astype(jnp.bfloat16)

    wide[...] = rows_product(grad_projected[...], weights[3])
    for strip in strips:
        grad_preact[strip] = (wide[strip] * slope[strip]).astype(jnp.bfloat16)
    grad_table = product(to_table, grad_preact[...])
    back[...] = grad_table[count:lookup_rows].astype(jnp.bfloat16)
    home = []
    for j, shift in enumerate(shifts):
        piece = pl.ds(j * halo_rows, halo_rows)
        home.append(send(back.at[piece], returned.at[piece], at_block(-shift)))
    grad_edge[...] = (grad_total[...] + rows_product(grad_preact[...], weights[1])).astype(jnp.bfloat16)
    new_node[...] = (node[...].astype(jnp.float32) + product(to_receiver, new_edge[...])).astype(jnp.bfloat16)
    grad_nodes = node_g[...].astype(jnp.float32) + rows_product(
        grad_table[lookup_rows:].astype(jnp.bfloat16), weights[2]
    )
    for copy in home:
        copy.wait_recv()
    grad_send = (grad_table[:count] + product(pick, returned[...])).astype(jnp.bfloat16)
    grad_node[...] = (grad_nodes + rows_product(grad_send, weights[0])).astype(jnp.bfloat16)
    for copy in sent:
        copy.wait_send()


def hand_out(*refs):
    copies = [pltpu.make_async_copy(refs[i], refs[4 + i], refs[8].at[i]) for i in range(4)]
    for copy in copies:
        copy.start()
    for copy in copies:
        copy.wait()


def solution(mesh):
    doms, mps = mesh.shape["dom"], mesh.shape["mp"]

    def shards(
        node_states, edge_states, edge_weight, send_weight, receive_weight, output_weight,
        norm_gain, senders, receivers, send_rows, node_cotangent, edge_cotangent,
    ):
        nodes, width = node_states.shape
        edges = edge_states.shape[0]
        hidden = edge_weight.shape[1]
        spread, halo_rows = send_rows.shape[1] // 2, send_rows.shape[2]
        halos = 2 * spread * halo_rows
        shifts = [step + 1 for step in range(spread)] + [-(step + 1) for step in range(spread)]
        square = mps == 4 and doms % 4 == 0 and edge_weight.shape[0] % 256 == 0
        copies = 4 * (13 if square else mps - 1) + 4 * spread
        any_space = pl.BlockSpec(memory_space=pl.ANY)
        bf16 = jnp.bfloat16
        results = pl.pallas_call(
            functools.partial(kernel, doms, mps, square, shifts),
            out_shape=(
                pltpu.VMEM((nodes, width), bf16),
                pltpu.VMEM((edges, width), bf16),
                pltpu.VMEM((nodes, width), bf16),
                pltpu.VMEM((edges, width), bf16),
            ),
            in_specs=[pl.BlockSpec(memory_space=pltpu.HBM)] * 12,
            out_specs=(pl.BlockSpec(memory_space=pltpu.VMEM),) * 4,
            scratch_shapes=[
                pltpu.VMEM((4, width, hidden), bf16),
                pltpu.VMEM((nodes, width), bf16),
                pltpu.VMEM((edges, width), bf16),
                pltpu.VMEM((1, width), jnp.float32),
                pltpu.VMEM((1, edges), jnp.int32),
                pltpu.VMEM((1, edges), jnp.int32),
                pltpu.VMEM(send_rows.shape, jnp.int32),
                pltpu.VMEM((nodes, width), bf16),
                pltpu.VMEM((edges, width), bf16),
                pltpu.VMEM((2 * nodes + halos, hidden), bf16),
                pltpu.VMEM((halos, hidden), bf16),
                pltpu.VMEM((halos, hidden), bf16),
                pltpu.VMEM((halos, hidden), bf16),
                pltpu.VMEM((edges, hidden), jnp.float32),
                pltpu.VMEM((edges, hidden), jnp.float32),
                pltpu.VMEM((edges, width), jnp.float32),
                pltpu.VMEM((edges, width), jnp.float32),
                pltpu.VMEM((edges, hidden), bf16),
                pltpu.VMEM((edges, width), bf16),
                pltpu.VMEM((edges, hidden), bf16),
                pltpu.SemaphoreType.DMA((12,)),
                pltpu.SemaphoreType.DMA((copies,)),
                pltpu.SemaphoreType.DMA((copies,)),
            ],
            compiler_params=pltpu.CompilerParams(
                collective_id=0, has_side_effects=True, vmem_limit_bytes=60 * 1024 * 1024
            ),
            cost_estimate=pl.CostEstimate(flops=2 * width * hidden * 4 * (nodes + edges), bytes_accessed=16 * width * hidden, transcendentals=edges * hidden),
        )(
            node_states, edge_states, edge_weight, send_weight, receive_weight, output_weight,
            norm_gain.reshape(1, width), senders.reshape(1, edges), receivers.reshape(1, edges),
            send_rows, node_cotangent, edge_cotangent,
        )
        return pl.pallas_call(
            hand_out,
            out_shape=tuple(jax.ShapeDtypeStruct(result.shape, bf16) for result in results),
            in_specs=[any_space] * 4,
            out_specs=(any_space,) * 4,
            scratch_shapes=[pltpu.SemaphoreType.DMA((4,))],
        )(*results)

    rows = P(("dom", "mp"), None)
    panel = P("mp", None)
    indices = P(("dom", "mp"))
    return jax.shard_map(
        shards,
        mesh=mesh,
        in_specs=(rows, rows, panel, panel, panel, panel, P(), indices, indices, P(("dom", "mp"), None, None), rows, rows),
        out_specs=(rows,) * 4,
        check_vma=False,
    )
```

```python
import functools

import jax
import jax.numpy as jnp
from jax import lax
from jax.experimental import pallas as pl
from jax.experimental.pallas import tpu as pltpu
from jax.sharding import PartitionSpec as P

eps = 1e-05
MESH = pl.DeviceIdType.MESH
OVER_Y = (
    (0, True), (1, True), (2, True), (3, True), (4, True), (5, True),
    (4, False), (5, False), (6, True), (7, True), (6, False), (7, False),
)
IN_FLIGHT = 3


def product(left, right):
    return jnp.dot(left, right, preferred_element_type=jnp.float32)


def rows_product(left, right):
    return lax.dot_general(
        left, right, (((1,), (1,)), ((), ())), preferred_element_type=jnp.float32
    )


def kernel(
    doms, mps, square, shifts,
    node_h, edge_h, edge_w, send_w, receive_w, output_w, gain_h, send_h, receive_h, rows_h, node_g_h, edge_g_h,
    new_node, new_edge, grad_node, grad_edge,
    weights, node, edge, gain, sender, receiver, rows, node_g, edge_g,
    table, halo, back, returned,
    wide, grad_table, slope, grad_total, scaled, hidden, grad_projected, grad_preact,
    load_sem, send_sem, recv_sem,
):
    dom, mp = lax.axis_index("dom"), lax.axis_index("mp")
    block = dom * mps + mp
    blocks = doms * mps
    count, halo_rows = node.shape[0], halo.shape[0] // len(shifts)
    panels = (send_w, edge_w, receive_w, output_w)
    size = send_w.shape[0]

    loads = []

    def load(source, target):
        copy = pltpu.make_async_copy(source, target, load_sem.at[len(loads)])
        copy.start()
        loads.append(copy)
        return copy

    own = pl.ds(pl.multiple_of(mp * size, size), size)
    load_panel = [load(panels[w], weights.at[w, own]) for w in range(4)]
    load_node = load(node_h, node)
    load_rows = load(rows_h, rows)
    load_sender = load(send_h, sender)
    load_receiver = load(receive_h, receiver)
    load_edge = load(edge_h, edge)
    load_gain = load(gain_h, gain)
    load_node_g = load(node_g_h, node_g)
    load_edge_g = load(edge_g_h, edge_g)

    def at_block(offset):
        other = lax.rem(block + offset + blocks, blocks)
        return (lax.div(other, mps), lax.rem(other, mps))

    if square:
        x, deep = lax.rem(dom, 2), lax.rem(lax.div(dom, 2), 2)
        core, y = lax.rem(mp, 2), lax.div(mp, 2)
        twin = (dom, mp + 1 - 2 * core)
        over_y = (dom, mp + 2 - 4 * y)
        over_x = (dom + 1 - 2 * x, mp)
        over_z = (dom + 2 - 4 * deep, mp)
        peers = [twin, over_y, over_x, over_z]
    else:
        peers = [(dom, lax.rem(mp + step, mps)) for step in range(1, mps)]
    barrier = pltpu.get_barrier_semaphore()
    greeted = peers + [at_block(shift) for shift in shifts]
    for peer in greeted:
        pl.semaphore_signal(barrier, inc=1, device_id=peer, device_id_type=MESH)
    pl.semaphore_wait(barrier, len(greeted))

    sent = []

    def send(source, target, peer):
        index = len(sent)
        copy = pltpu.make_async_remote_copy(
            src_ref=source, dst_ref=target, send_sem=send_sem.at[index], recv_sem=recv_sem.at[index],
            device_id=peer, device_id_type=MESH,
        )
        copy.start()
        sent.append(copy)
        return copy

    if square:
        quarter = size // 4
        half = quarter // 2
        mine = x + 2 * deep
        by_x, by_z, opposite = mine + 1 - 2 * x, mine + 2 - 4 * deep, 3 - mine
        far = (mp + 2 - 4 * y) * size
        near = mp * size

        def part(w, start, length):
            return weights.at[w, pl.ds(pl.multiple_of(start, 16), length)]

        def place(piece, which):
            return which * quarter + (piece % 2) * half

        A = [None] * 4
        Y = [None] * len(OVER_Y)
        X, Z, DX, DZ, SB, SX, SZ, SD = ([None] * 8 for _ in range(8))

        def begin_twin(w):
            A[w] = send(panels[w], weights.at[w, own], twin)

        def begin(step):
            piece, direct = OVER_Y[step]
            start = place(piece, mine if direct else opposite)
            Y[step] = send(
                panels[piece // 2].at[pl.ds(pl.multiple_of(start, 16), half)],
                part(piece // 2, near + start, half), over_y,
            )

        def forward(piece, which, peer, start=0, length=half):
            region = part(piece // 2, far + place(piece, which) + start, length)
            return send(region, region, peer)

        def arrive_y(step):
            piece, direct = OVER_Y[step]
            Y[step].wait_recv()
            if direct:
                X[piece] = forward(piece, mine, over_x)
                Z[piece] = forward(piece, mine, over_z)
            if step + IN_FLIGHT < len(OVER_Y):
                begin(step + IN_FLIGHT)
            if direct:
                SB[piece] = forward(piece, mine, twin)
            else:
                SD[piece] = forward(piece, opposite, twin)

        def arrive_plane(piece):
            X[piece].wait_recv()
            if piece < 4:
                DZ[piece] = forward(piece, by_x, over_z, half // 2, half // 2)
            SX[piece] = forward(piece, by_x, twin)
            Z[piece].wait_recv()
            if piece < 4:
                DX[piece] = forward(piece, by_z, over_x, 0, half // 2)
            SZ[piece] = forward(piece, by_z, twin)

        def arrive_opposite(piece):
            DX[piece].wait_recv()
            DZ[piece].wait_recv()
            SD[piece] = forward(piece, opposite, twin)

        def complete(w):
            load_panel[w].wait()
            A[w].wait_recv()
            for piece in (2 * w, 2 * w + 1):
                for copy in (SB[piece], SX[piece], SZ[piece], SD[piece]):
                    copy.wait_recv()
    else:
        direct = [[send(panels[w], weights.at[w, own], peer) for peer in peers] for w in range(4)]

        def complete(w):
            load_panel[w].wait()
            for copy in direct[w]:
                copy.wait_recv()

    def project_send():
        load_node.wait()
        load_rows.wait()
        chosen = jnp.concatenate([rows[0, j : j + 1, :] for j in range(len(shifts))], axis=1)
        table[:count] = product(node[...], weights[0]).astype(jnp.bfloat16)
        pick = (lax.broadcasted_iota(jnp.int32, (count, halo.shape[0]), 0) == chosen).astype(jnp.float32)
        halo[...] = product(pick.T.astype(jnp.bfloat16), table[:count]).astype(jnp.bfloat16)
        arrive = []
        for j, shift in enumerate(shifts):
            arrive.append(send(
                halo.at[pl.ds(j * halo_rows, halo_rows)],
                table.at[pl.ds(count + j * halo_rows, halo_rows)], at_block(shift),
            ))
        return pick.astype(jnp.bfloat16), arrive

    lookup_rows = count + halo.shape[0]

    def project_receive():
        table[lookup_rows:] = product(node[...], weights[2]).astype(jnp.bfloat16)

    if square:
        for step in range(IN_FLIGHT):
            begin(step)
        begin_twin(0)
        begin_twin(1)
    for copy in (load_edge, load_sender, load_receiver, load_gain, load_node_g, load_edge_g):
        copy.wait()
    edges = edge.shape[0]
    by_sender = lax.broadcasted_iota(jnp.int32, (lookup_rows, edges), 0) == sender[...]
    by_receiver = lax.broadcasted_iota(jnp.int32, (count, edges), 0) == receiver[...]
    to_table = jnp.concatenate([by_sender.astype(jnp.float32), by_receiver.astype(jnp.float32)], axis=0)
    from_table = to_table.T.astype(jnp.bfloat16)
    to_receiver = by_receiver.astype(jnp.float32)
    from_receiver = to_receiver.T.astype(jnp.bfloat16)
    to_table = to_table.astype(jnp.bfloat16)
    to_receiver = to_receiver.astype(jnp.bfloat16)

    strips = [pl.ds(start, 16) for start in range(0, edges, 16)]
    grad_total[...] = edge_g[...].astype(jnp.float32) + product(from_receiver, node_g[...])
    for strip in strips:
        values = grad_total[strip] * gain[...]
        scaled[strip] = values - jnp.mean(values, axis=-1, keepdims=True)
    bands = [pl.ds(start, 256) for start in range(0, wide.shape[1], 256)]

    def project_edge():
        for band in bands:
            wide[:, band] = product(edge[...], weights[1, :, band])

    if square:
        arrive_y(0)
        arrive_y(1)
        begin_twin(2)
        arrive_plane(0)
        arrive_y(2)
        begin_twin(3)
        arrive_plane(1)
        arrive_y(3)
        arrive_opposite(0)
        arrive_y(4)
        arrive_plane(2)
        arrive_opposite(1)
        arrive_y(5)
        arrive_plane(3)
        complete(0)
        pick, arrive = project_send()
        arrive_opposite(2)
        arrive_y(6)
        arrive_plane(4)
        arrive_opposite(3)
        arrive_y(7)
        arrive_plane(5)
        arrive_y(8)
        complete(1)
        project_edge()
        arrive_y(9)
        arrive_y(10)
        arrive_plane(6)
        complete(2)
        project_receive()
        arrive_y(11)
        arrive_plane(7)
    else:
        complete(0)
        pick, arrive = project_send()
        complete(1)
        project_edge()
        complete(2)
        project_receive()

    for copy in arrive:
        copy.wait_recv()
    for band in bands:
        values = wide[:, band] + product(from_table, table[:, band])
        sigmoid = jax.nn.sigmoid(values)
        hidden[:, band] = (values * sigmoid).astype(jnp.bfloat16)
        slope[:, band] = sigmoid * (1.0 + values * (1.0 - sigmoid))

    complete(3)
    for band in bands:
        wide[:, band] = product(hidden[...], weights[3, :, band])
    for strip in strips:
        values = wide[strip]
        centred = values - jnp.mean(values, axis=-1, keepdims=True)
        variance = jnp.mean(centred * centred, axis=-1, keepdims=True)
        along = jnp.mean(scaled[strip] * centred, axis=-1, keepdims=True)
        scale = lax.rsqrt(variance + eps)
        unit_rows = centred * scale
        new_edge[strip] = (edge[strip].astype(jnp.float32) + unit_rows * gain[...]).astype(jnp.bfloat16)
        grad_projected[strip] = (scale * (scaled[strip] - unit_rows * (scale * along))).astype(jnp.bfloat16)

    for band in bands:
        values = rows_product(grad_projected[...], weights[3, band]) * slope[:, band]
        grad_preact[:, band] = values.astype(jnp.bfloat16)
        grad_table[:, band] = product(to_table, grad_preact[:, band])
    back[...] = grad_table[count:lookup_rows].astype(jnp.bfloat16)
    home = []
    for j, shift in enumerate(shifts):
        piece = pl.ds(j * halo_rows, halo_rows)
        home.append(send(back.at[piece], returned.at[piece], at_block(-shift)))
    for band in bands:
        values = grad_total[:, band] + rows_product(grad_preact[...], weights[1, band])
        grad_edge[:, band] = values.astype(jnp.bfloat16)
    new_node[...] = (node[...].astype(jnp.float32) + product(to_receiver, new_edge[...])).astype(jnp.bfloat16)
    grad_nodes = node_g[...].astype(jnp.float32) + rows_product(
        grad_table[lookup_rows:].astype(jnp.bfloat16), weights[2]
    )
    for copy in home:
        copy.wait_recv()
    grad_send = (grad_table[:count] + product(pick, returned[...])).astype(jnp.bfloat16)
    grad_node[...] = (grad_nodes + rows_product(grad_send, weights[0])).astype(jnp.bfloat16)
    for copy in sent:
        copy.wait_send()


def hand_out(*refs):
    copies = [pltpu.make_async_copy(refs[i], refs[4 + i], refs[8].at[i]) for i in range(4)]
    for copy in copies:
        copy.start()
    for copy in copies:
        copy.wait()


def solution(mesh):
    doms, mps = mesh.shape["dom"], mesh.shape["mp"]

    def shards(
        node_states, edge_states, edge_weight, send_weight, receive_weight, output_weight,
        norm_gain, senders, receivers, send_rows, node_cotangent, edge_cotangent,
    ):
        nodes, width = node_states.shape
        edges = edge_states.shape[0]
        hidden = edge_weight.shape[1]
        spread, halo_rows = send_rows.shape[1] // 2, send_rows.shape[2]
        halos = 2 * spread * halo_rows
        shifts = [step + 1 for step in range(spread)] + [-(step + 1) for step in range(spread)]
        square = mps == 4 and doms % 4 == 0 and edge_weight.shape[0] % 256 == 0
        copies = (72 if square else 4 * (mps - 1)) + 4 * spread
        any_space = pl.BlockSpec(memory_space=pl.ANY)
        bf16 = jnp.bfloat16
        results = pl.pallas_call(
            functools.partial(kernel, doms, mps, square, shifts),
            out_shape=(
                pltpu.VMEM((nodes, width), bf16),
                pltpu.VMEM((edges, width), bf16),
                pltpu.VMEM((nodes, width), bf16),
                pltpu.VMEM((edges, width), bf16),
            ),
            in_specs=[pl.BlockSpec(memory_space=pltpu.HBM)] * 12,
            out_specs=(pl.BlockSpec(memory_space=pltpu.VMEM),) * 4,
            scratch_shapes=[
                pltpu.VMEM((4, width, hidden), bf16),
                pltpu.VMEM((nodes, width), bf16),
                pltpu.VMEM((edges, width), bf16),
                pltpu.VMEM((1, width), jnp.float32),
                pltpu.VMEM((1, edges), jnp.int32),
                pltpu.VMEM((1, edges), jnp.int32),
                pltpu.VMEM(send_rows.shape, jnp.int32),
                pltpu.VMEM((nodes, width), bf16),
                pltpu.VMEM((edges, width), bf16),
                pltpu.VMEM((2 * nodes + halos, hidden), bf16),
                pltpu.VMEM((halos, hidden), bf16),
                pltpu.VMEM((halos, hidden), bf16),
                pltpu.VMEM((halos, hidden), bf16),
                pltpu.VMEM((edges, hidden), jnp.float32),
                pltpu.VMEM((2 * nodes + halos, hidden), jnp.float32),
                pltpu.VMEM((edges, hidden), jnp.float32),
                pltpu.VMEM((edges, width), jnp.float32),
                pltpu.VMEM((edges, width), jnp.float32),
                pltpu.VMEM((edges, hidden), bf16),
                pltpu.VMEM((edges, width), bf16),
                pltpu.VMEM((edges, hidden), bf16),
                pltpu.SemaphoreType.DMA((12,)),
                pltpu.SemaphoreType.DMA((copies,)),
                pltpu.SemaphoreType.DMA((copies,)),
            ],
            compiler_params=pltpu.CompilerParams(
                collective_id=0, has_side_effects=True, vmem_limit_bytes=60 * 1024 * 1024
            ),
            cost_estimate=pl.CostEstimate(flops=2 * width * hidden * 4 * (nodes + edges), bytes_accessed=16 * width * hidden, transcendentals=edges * hidden),
        )(
            node_states, edge_states, edge_weight, send_weight, receive_weight, output_weight,
            norm_gain.reshape(1, width), senders.reshape(1, edges), receivers.reshape(1, edges),
            send_rows, node_cotangent, edge_cotangent,
        )
        return pl.pallas_call(
            hand_out,
            out_shape=tuple(jax.ShapeDtypeStruct(result.shape, bf16) for result in results),
            in_specs=[pl.BlockSpec(memory_space=pltpu.VMEM)] * 4,
            out_specs=(any_space,) * 4,
            scratch_shapes=[pltpu.SemaphoreType.DMA((4,))],
            compiler_params=pltpu.CompilerParams(vmem_limit_bytes=8 * 1024 * 1024),
        )(*results)

    rows = P(("dom", "mp"), None)
    panel = P("mp", None)
    indices = P(("dom", "mp"))
    return jax.shard_map(
        shards,
        mesh=mesh,
        in_specs=(rows, rows, panel, panel, panel, panel, P(), indices, indices, P(("dom", "mp"), None, None), rows, rows),
        out_specs=(rows,) * 4,
        check_vma=False,
    )
```

```python
import functools

import jax
import jax.numpy as jnp
from jax import lax
from jax.experimental import pallas as pl
from jax.experimental.pallas import tpu as pltpu
from jax.sharding import PartitionSpec as P

eps = 1e-05
MESH = pl.DeviceIdType.MESH
DIAGONAL = ((0, 2, 2), (0, 2, 2), (4, 0, 0), (4, 0, 0))


def product(left, right):
    return jnp.dot(left, right, preferred_element_type=jnp.float32)


def rows_product(left, right):
    return lax.dot_general(
        left, right, (((1,), (1,)), ((), ())), preferred_element_type=jnp.float32
    )


def kernel(
    doms, mps, square, shifts,
    node_h, edge_h, edge_w, send_w, receive_w, output_w, gain_h, send_h, receive_h, rows_h, node_g_h, edge_g_h,
    new_node, new_edge, grad_node, grad_edge,
    weights, node, edge, gain, sender, receiver, rows, node_g, edge_g,
    table, halo, back, returned,
    wide, grad_table, slope, grad_total, scaled, hidden, grad_projected, grad_preact,
    load_sem, send_sem, recv_sem,
):
    dom, mp = lax.axis_index("dom"), lax.axis_index("mp")
    block = dom * mps + mp
    blocks = doms * mps
    count, halo_rows = node.shape[0], halo.shape[0] // len(shifts)
    panels = (send_w, edge_w, receive_w, output_w)
    size = send_w.shape[0]

    loads = []

    def load(source, target):
        copy = pltpu.make_async_copy(source, target, load_sem.at[len(loads)])
        copy.start()
        loads.append(copy)
        return copy

    own = pl.ds(pl.multiple_of(mp * size, size), size)
    load_panel = [load(panels[w], weights.at[w, own]) for w in range(4)]
    load_node = load(node_h, node)
    load_rows = load(rows_h, rows)
    load_sender = load(send_h, sender)
    load_receiver = load(receive_h, receiver)
    load_edge = load(edge_h, edge)
    load_gain = load(gain_h, gain)
    load_node_g = load(node_g_h, node_g)
    load_edge_g = load(edge_g_h, edge_g)

    def at_block(offset):
        other = lax.rem(block + offset + blocks, blocks)
        return (lax.div(other, mps), lax.rem(other, mps))

    if square:
        x, deep = lax.rem(dom, 2), lax.rem(lax.div(dom, 2), 2)
        core, y = lax.rem(mp, 2), lax.div(mp, 2)
        twin = (dom, mp + 1 - 2 * core)
        over_y = (dom, mp + 2 - 4 * y)
        over_x = (dom + 1 - 2 * x, mp)
        over_z = (dom + 2 - 4 * deep, mp)
        peers = [twin, over_y, over_x, over_z]
    else:
        peers = [(dom, lax.rem(mp + step, mps)) for step in range(1, mps)]
    barrier = pltpu.get_barrier_semaphore()
    greeted = peers + [at_block(shift) for shift in shifts]
    for peer in greeted:
        pl.semaphore_signal(barrier, inc=1, device_id=peer, device_id_type=MESH)
    pl.semaphore_wait(barrier, len(greeted))

    sent = []

    def send(source, target, peer):
        index = len(sent)
        copy = pltpu.make_async_remote_copy(
            src_ref=source, dst_ref=target, send_sem=send_sem.at[index], recv_sem=recv_sem.at[index],
            device_id=peer, device_id_type=MESH,
        )
        copy.start()
        sent.append(copy)
        return copy

    if square:
        unit = size // 16
        quarter = size // 4
        mine = x + 2 * deep
        by_x, by_z, opposite = mine + 1 - 2 * x, mine + 2 - 4 * deep, 3 - mine
        far = (mp + 2 - 4 * y) * size
        near = mp * size

        def part(w, base, start, length):
            return weights.at[w, pl.ds(pl.multiple_of(base + start, unit), length)]

        A, B, DY, X, Z, DX, DZ, SB, SX, SZ, SD = ([None] * 4 for _ in range(11))

        def begin_twin(w):
            A[w] = send(panels[w], weights.at[w, own], twin)

        def begin(w):
            B[w] = send(
                panels[w].at[pl.ds(pl.multiple_of(mine * quarter, quarter), quarter)],
                part(w, near, mine * quarter, quarter), over_y,
            )

        def begin_diagonal(w):
            length = DIAGONAL[w][0] * unit
            DY[w] = send(
                panels[w].at[pl.ds(pl.multiple_of(opposite * quarter, quarter), length)],
                part(w, near, opposite * quarter, length), over_y,
            )

        def forward(w, start, length, peer):
            region = part(w, far, start, length)
            return send(region, region, peer)

        def step1(w):
            B[w].wait_recv()
            X[w] = forward(w, mine * quarter, quarter, over_x)
            Z[w] = forward(w, mine * quarter, quarter, over_z)
            if w == 0:
                begin(2)
            elif w == 1:
                begin(3)
            else:
                begin_diagonal(w)
            SB[w] = forward(w, mine * quarter, quarter, twin)

        def step2(w):
            dy, dx, dz = (units * unit for units in DIAGONAL[w])
            X[w].wait_recv()
            if dz:
                DZ[w] = forward(w, by_x * quarter + dy + dx, dz, over_z)
            SX[w] = forward(w, by_x * quarter, quarter, twin)
            Z[w].wait_recv()
            if dx:
                DX[w] = forward(w, by_z * quarter + dy, dx, over_x)
            SZ[w] = forward(w, by_z * quarter, quarter, twin)

        def step3(w):
            for copy in (DY[w], DX[w], DZ[w]):
                if copy is not None:
                    copy.wait_recv()
            SD[w] = forward(w, opposite * quarter, quarter, twin)

        def step4(w):
            load_panel[w].wait()
            for copy in (A[w], SB[w], SX[w], SZ[w], SD[w]):
                copy.wait_recv()
    else:
        direct = [[send(panels[w], weights.at[w, own], peer) for peer in peers] for w in range(4)]

        def step4(w):
            load_panel[w].wait()
            for copy in direct[w]:
                copy.wait_recv()

    def project_send():
        load_node.wait()
        load_rows.wait()
        chosen = jnp.concatenate([rows[0, j : j + 1, :] for j in range(len(shifts))], axis=1)
        table[:count] = product(node[...], weights[0]).astype(jnp.bfloat16)
        pick = (lax.broadcasted_iota(jnp.int32, (count, halo.shape[0]), 0) == chosen).astype(jnp.float32)
        halo[...] = product(pick.T.astype(jnp.bfloat16), table[:count]).astype(jnp.bfloat16)
        arrive = []
        for j, shift in enumerate(shifts):
            arrive.append(send(
                halo.at[pl.ds(j * halo_rows, halo_rows)],
                table.at[pl.ds(count + j * halo_rows, halo_rows)], at_block(shift),
            ))
        return pick.astype(jnp.bfloat16), arrive

    lookup_rows = count + halo.shape[0]

    def project_receive():
        table[lookup_rows:] = product(node[...], weights[2]).astype(jnp.bfloat16)

    if square:
        begin(0)
        begin(1)
        begin_twin(0)
        begin_twin(1)
    for copy in (load_edge, load_sender, load_receiver, load_gain, load_node_g, load_edge_g):
        copy.wait()
    edges = edge.shape[0]
    by_sender = lax.broadcasted_iota(jnp.int32, (lookup_rows, edges), 0) == sender[...]
    by_receiver = lax.broadcasted_iota(jnp.int32, (count, edges), 0) == receiver[...]
    to_table = jnp.concatenate([by_sender.astype(jnp.float32), by_receiver.astype(jnp.float32)], axis=0)
    from_table = to_table.T.astype(jnp.bfloat16)
    to_receiver = by_receiver.astype(jnp.float32)
    from_receiver = to_receiver.T.astype(jnp.bfloat16)
    to_table = to_table.astype(jnp.bfloat16)
    to_receiver = to_receiver.astype(jnp.bfloat16)

    strips = [pl.ds(start, 16) for start in range(0, edges, 16)]
    grad_total[...] = edge_g[...].astype(jnp.float32) + product(from_receiver, node_g[...])
    for strip in strips:
        values = grad_total[strip] * gain[...]
        scaled[strip] = values - jnp.mean(values, axis=-1, keepdims=True)
    bands = [pl.ds(start, 256) for start in range(0, wide.shape[1], 256)]

    def project_edge():
        for band in bands:
            wide[:, band] = product(edge[...], weights[1, :, band])

    if square:
        step1(0)
        begin_twin(2)
        step1(1)
        begin_twin(3)
        step2(0)
        step1(2)
        step2(1)
        step3(0)
        step1(3)
        step4(0)
        pick, arrive = project_send()
        step2(2)
        step3(1)
        step4(1)
        project_edge()
        step3(2)
        step2(3)
        step3(3)
        step4(2)
        project_receive()
    else:
        step4(0)
        pick, arrive = project_send()
        step4(1)
        project_edge()
        step4(2)
        project_receive()

    for copy in arrive:
        copy.wait_recv()
    for band in bands:
        values = wide[:, band] + product(from_table, table[:, band])
        sigmoid = jax.nn.sigmoid(values)
        hidden[:, band] = (values * sigmoid).astype(jnp.bfloat16)
        slope[:, band] = sigmoid * (1.0 + values * (1.0 - sigmoid))

    step4(3)
    for band in bands:
        wide[:, band] = product(hidden[...], weights[3, :, band])
    for strip in strips:
        values = wide[strip]
        centred = values - jnp.mean(values, axis=-1, keepdims=True)
        variance = jnp.mean(centred * centred, axis=-1, keepdims=True)
        along = jnp.mean(scaled[strip] * centred, axis=-1, keepdims=True)
        scale = lax.rsqrt(variance + eps)
        unit_rows = centred * scale
        new_edge[strip] = (edge[strip].astype(jnp.float32) + unit_rows * gain[...]).astype(jnp.bfloat16)
        grad_projected[strip] = (scale * (scaled[strip] - unit_rows * (scale * along))).astype(jnp.bfloat16)

    for band in bands:
        values = rows_product(grad_projected[...], weights[3, band]) * slope[:, band]
        grad_preact[:, band] = values.astype(jnp.bfloat16)
        grad_table[:, band] = product(to_table, grad_preact[:, band])
    back[...] = grad_table[count:lookup_rows].astype(jnp.bfloat16)
    home = []
    for j, shift in enumerate(shifts):
        piece = pl.ds(j * halo_rows, halo_rows)
        home.append(send(back.at[piece], returned.at[piece], at_block(-shift)))
    for band in bands:
        values = grad_total[:, band] + rows_product(grad_preact[...], weights[1, band])
        grad_edge[:, band] = values.astype(jnp.bfloat16)
    new_node[...] = (node[...].astype(jnp.float32) + product(to_receiver, new_edge[...])).astype(jnp.bfloat16)
    grad_nodes = node_g[...].astype(jnp.float32) + rows_product(
        grad_table[lookup_rows:].astype(jnp.bfloat16), weights[2]
    )
    for copy in home:
        copy.wait_recv()
    grad_send = (grad_table[:count] + product(pick, returned[...])).astype(jnp.bfloat16)
    grad_node[...] = (grad_nodes + rows_product(grad_send, weights[0])).astype(jnp.bfloat16)
    for copy in sent:
        copy.wait_send()


def hand_out(*refs):
    copies = [pltpu.make_async_copy(refs[i], refs[4 + i], refs[8].at[i]) for i in range(4)]
    for copy in copies:
        copy.start()
    for copy in copies:
        copy.wait()


def solution(mesh):
    doms, mps = mesh.shape["dom"], mesh.shape["mp"]

    def shards(
        node_states, edge_states, edge_weight, send_weight, receive_weight, output_weight,
        norm_gain, senders, receivers, send_rows, node_cotangent, edge_cotangent,
    ):
        nodes, width = node_states.shape
        edges = edge_states.shape[0]
        hidden = edge_weight.shape[1]
        spread, halo_rows = send_rows.shape[1] // 2, send_rows.shape[2]
        halos = 2 * spread * halo_rows
        shifts = [step + 1 for step in range(spread)] + [-(step + 1) for step in range(spread)]
        square = mps == 4 and doms % 4 == 0 and edge_weight.shape[0] % 256 == 0
        copies = (38 if square else 4 * (mps - 1)) + 4 * spread
        any_space = pl.BlockSpec(memory_space=pl.ANY)
        bf16 = jnp.bfloat16
        results = pl.pallas_call(
            functools.partial(kernel, doms, mps, square, shifts),
            out_shape=(
                pltpu.VMEM((nodes, width), bf16),
                pltpu.VMEM((edges, width), bf16),
                pltpu.VMEM((nodes, width), bf16),
                pltpu.VMEM((edges, width), bf16),
            ),
            in_specs=[pl.BlockSpec(memory_space=pltpu.HBM)] * 12,
            out_specs=(pl.BlockSpec(memory_space=pltpu.VMEM),) * 4,
            scratch_shapes=[
                pltpu.VMEM((4, width, hidden), bf16),
                pltpu.VMEM((nodes, width), bf16),
                pltpu.VMEM((edges, width), bf16),
                pltpu.VMEM((1, width), jnp.float32),
                pltpu.VMEM((1, edges), jnp.int32),
                pltpu.VMEM((1, edges), jnp.int32),
                pltpu.VMEM(send_rows.shape, jnp.int32),
                pltpu.VMEM((nodes, width), bf16),
                pltpu.VMEM((edges, width), bf16),
                pltpu.VMEM((2 * nodes + halos, hidden), bf16),
                pltpu.VMEM((halos, hidden), bf16),
                pltpu.VMEM((halos, hidden), bf16),
                pltpu.VMEM((halos, hidden), bf16),
                pltpu.VMEM((edges, hidden), jnp.float32),
                pltpu.VMEM((2 * nodes + halos, hidden), jnp.float32),
                pltpu.VMEM((edges, hidden), jnp.float32),
                pltpu.VMEM((edges, width), jnp.float32),
                pltpu.VMEM((edges, width), jnp.float32),
                pltpu.VMEM((edges, hidden), bf16),
                pltpu.VMEM((edges, width), bf16),
                pltpu.VMEM((edges, hidden), bf16),
                pltpu.SemaphoreType.DMA((12,)),
                pltpu.SemaphoreType.DMA((copies,)),
                pltpu.SemaphoreType.DMA((copies,)),
            ],
            compiler_params=pltpu.CompilerParams(
                collective_id=0, has_side_effects=True, vmem_limit_bytes=60 * 1024 * 1024
            ),
            cost_estimate=pl.CostEstimate(flops=2 * width * hidden * 4 * (nodes + edges), bytes_accessed=16 * width * hidden, transcendentals=edges * hidden),
        )(
            node_states, edge_states, edge_weight, send_weight, receive_weight, output_weight,
            norm_gain.reshape(1, width), senders.reshape(1, edges), receivers.reshape(1, edges),
            send_rows, node_cotangent, edge_cotangent,
        )
        return pl.pallas_call(
            hand_out,
            out_shape=tuple(jax.ShapeDtypeStruct(result.shape, bf16) for result in results),
            in_specs=[pl.BlockSpec(memory_space=pltpu.VMEM)] * 4,
            out_specs=(any_space,) * 4,
            scratch_shapes=[pltpu.SemaphoreType.DMA((4,))],
            compiler_params=pltpu.CompilerParams(vmem_limit_bytes=8 * 1024 * 1024),
        )(*results)

    rows = P(("dom", "mp"), None)
    panel = P("mp", None)
    indices = P(("dom", "mp"))
    return jax.shard_map(
        shards,
        mesh=mesh,
        in_specs=(rows, rows, panel, panel, panel, panel, P(), indices, indices, P(("dom", "mp"), None, None), rows, rows),
        out_specs=(rows,) * 4,
        check_vma=False,
    )
```

```python
import functools

import jax
import jax.numpy as jnp
from jax import lax
from jax.experimental import pallas as pl
from jax.experimental.pallas import tpu as pltpu
from jax.sharding import PartitionSpec as P

eps = 1e-05
MESH = pl.DeviceIdType.MESH
DIAGONAL = ((0, 2, 2), (0, 2, 2), (4, 0, 0), (4, 0, 0))


def product(left, right):
    return jnp.dot(left, right, preferred_element_type=jnp.float32)


def rows_product(left, right):
    return lax.dot_general(
        left, right, (((1,), (1,)), ((), ())), preferred_element_type=jnp.float32
    )


def kernel(
    doms, mps, square, shifts,
    node_h, edge_h, edge_w, send_w, receive_w, output_w, gain_h, send_h, receive_h, rows_h, node_g_h, edge_g_h,
    new_node, new_edge, grad_node, grad_edge,
    weights, node, edge, gain, sender, receiver, rows, node_g, edge_g,
    table, halo, back, returned,
    wide, slope, grad_total, scaled, hidden, grad_projected, grad_preact,
    load_sem, send_sem, recv_sem,
):
    dom, mp = lax.axis_index("dom"), lax.axis_index("mp")
    block = dom * mps + mp
    blocks = doms * mps
    count, halo_rows = node.shape[0], halo.shape[0] // len(shifts)
    panels = (send_w, edge_w, receive_w, output_w)
    size = send_w.shape[0]

    loads = []

    def load(source, target):
        copy = pltpu.make_async_copy(source, target, load_sem.at[len(loads)])
        copy.start()
        loads.append(copy)
        return copy

    own = pl.ds(pl.multiple_of(mp * size, size), size)
    load_panel = [load(panels[w], weights.at[w, own]) for w in range(4)]
    load_node = load(node_h, node)
    load_rows = load(rows_h, rows)
    load_sender = load(send_h, sender)
    load_receiver = load(receive_h, receiver)
    load_edge = load(edge_h, edge)
    load_gain = load(gain_h, gain)
    load_node_g = load(node_g_h, node_g)
    load_edge_g = load(edge_g_h, edge_g)

    def at_block(offset):
        other = lax.rem(block + offset + blocks, blocks)
        return (lax.div(other, mps), lax.rem(other, mps))

    if square:
        x, deep = lax.rem(dom, 2), lax.rem(lax.div(dom, 2), 2)
        core, y = lax.rem(mp, 2), lax.div(mp, 2)
        twin = (dom, mp + 1 - 2 * core)
        over_y = (dom, mp + 2 - 4 * y)
        over_x = (dom + 1 - 2 * x, mp)
        over_z = (dom + 2 - 4 * deep, mp)
        peers = [twin, over_y, over_x, over_z]
    else:
        peers = [(dom, lax.rem(mp + step, mps)) for step in range(1, mps)]
    barrier = pltpu.get_barrier_semaphore()
    greeted = peers + [at_block(shift) for shift in shifts]
    for peer in greeted:
        pl.semaphore_signal(barrier, inc=1, device_id=peer, device_id_type=MESH)
    pl.semaphore_wait(barrier, len(greeted))

    sent = []

    def send(source, target, peer):
        index = len(sent)
        copy = pltpu.make_async_remote_copy(
            src_ref=source, dst_ref=target, send_sem=send_sem.at[index], recv_sem=recv_sem.at[index],
            device_id=peer, device_id_type=MESH,
        )
        copy.start()
        sent.append(copy)
        return copy

    if square:
        unit = size // 16
        quarter = size // 4
        mine = x + 2 * deep
        by_x, by_z, opposite = mine + 1 - 2 * x, mine + 2 - 4 * deep, 3 - mine
        far = (mp + 2 - 4 * y) * size
        near = mp * size

        def part(w, base, start, length):
            return weights.at[w, pl.ds(pl.multiple_of(base + start, unit), length)]

        A, B, DY, X, Z, DX, DZ, SB, SX, SZ, SD = ([None] * 4 for _ in range(11))

        def begin_twin(w):
            A[w] = send(panels[w], weights.at[w, own], twin)

        def begin(w):
            B[w] = send(
                panels[w].at[pl.ds(pl.multiple_of(mine * quarter, quarter), quarter)],
                part(w, near, mine * quarter, quarter), over_y,
            )

        def begin_diagonal(w):
            length = DIAGONAL[w][0] * unit
            DY[w] = send(
                panels[w].at[pl.ds(pl.multiple_of(opposite * quarter, quarter), length)],
                part(w, near, opposite * quarter, length), over_y,
            )

        def forward(w, start, length, peer):
            region = part(w, far, start, length)
            return send(region, region, peer)

        def step1(w):
            B[w].wait_recv()
            X[w] = forward(w, mine * quarter, quarter, over_x)
            Z[w] = forward(w, mine * quarter, quarter, over_z)
            if w == 0:
                begin(2)
            elif w == 1:
                begin(3)
            else:
                begin_diagonal(w)
            if w >= 2:
                SB[w] = forward(w, mine * quarter, quarter, twin)

        def step2(w):
            dy, dx, dz = (units * unit for units in DIAGONAL[w])
            X[w].wait_recv()
            if dz:
                DZ[w] = forward(w, by_x * quarter + dy + dx, dz, over_z)
            if w >= 2:
                SX[w] = forward(w, by_x * quarter, quarter, twin)
            Z[w].wait_recv()
            if dx:
                DX[w] = forward(w, by_z * quarter + dy, dx, over_x)
            if w >= 2:
                SZ[w] = forward(w, by_z * quarter, quarter, twin)

        def step3(w):
            for copy in (DY[w], DX[w], DZ[w]):
                if copy is not None:
                    copy.wait_recv()
            if w >= 2:
                SD[w] = forward(w, opposite * quarter, quarter, twin)
            else:
                SD[w] = forward(w, 0, size, twin)

        def step4(w):
            load_panel[w].wait()
            for copy in (A[w], SB[w], SX[w], SZ[w], SD[w]):
                if copy is not None:
                    copy.wait_recv()
    else:
        direct = [[send(panels[w], weights.at[w, own], peer) for peer in peers] for w in range(4)]

        def step4(w):
            load_panel[w].wait()
            for copy in direct[w]:
                copy.wait_recv()

    def project_send():
        load_node.wait()
        load_rows.wait()
        chosen = jnp.concatenate([rows[0, j : j + 1, :] for j in range(len(shifts))], axis=1)
        table[:count] = product(node[...], weights[0]).astype(jnp.bfloat16)
        pick = (lax.broadcasted_iota(jnp.int32, (count, halo.shape[0]), 0) == chosen).astype(jnp.float32)
        halo[...] = product(pick.T.astype(jnp.bfloat16), table[:count]).astype(jnp.bfloat16)
        arrive = []
        for j, shift in enumerate(shifts):
            arrive.append(send(
                halo.at[pl.ds(j * halo_rows, halo_rows)],
                table.at[pl.ds(count + j * halo_rows, halo_rows)], at_block(shift),
            ))
        return pick.astype(jnp.bfloat16), arrive

    lookup_rows = count + halo.shape[0]

    def project_receive():
        table[lookup_rows:] = product(node[...], weights[2]).astype(jnp.bfloat16)

    if square:
        begin(0)
        begin(1)
        begin_twin(0)
        begin_twin(1)
    for copy in (load_edge, load_sender, load_receiver, load_gain, load_node_g, load_edge_g):
        copy.wait()
    edges = edge.shape[0]
    by_sender = lax.broadcasted_iota(jnp.int32, (lookup_rows, edges), 0) == sender[...]
    by_receiver = lax.broadcasted_iota(jnp.int32, (count, edges), 0) == receiver[...]
    to_table = jnp.concatenate([by_sender.astype(jnp.float32), by_receiver.astype(jnp.float32)], axis=0)
    from_table = to_table.T.astype(jnp.bfloat16)
    to_receiver = by_receiver.astype(jnp.float32)
    from_receiver = to_receiver.T.astype(jnp.bfloat16)
    to_table = to_table.astype(jnp.bfloat16)
    to_receiver = to_receiver.astype(jnp.bfloat16)

    strips = [pl.ds(start, 16) for start in range(0, edges, 16)]
    grad_total[...] = edge_g[...].astype(jnp.float32) + product(from_receiver, node_g[...])
    for strip in strips:
        values = grad_total[strip] * gain[...]
        scaled[strip] = values - jnp.mean(values, axis=-1, keepdims=True)
    if square:
        step1(0)
        begin_twin(2)
        step1(1)
        begin_twin(3)
        step2(0)
        step1(2)
        step2(1)
        step3(0)
        step1(3)
        step2(2)
        step4(0)
        pick, arrive = project_send()
        step3(1)
        step3(2)
        step4(1)
        wide[...] = product(edge[...], weights[1])
        step2(3)
        step3(3)
        step4(2)
    else:
        step4(0)
        pick, arrive = project_send()
        step4(1)
        wide[...] = product(edge[...], weights[1])
        step4(2)
    project_receive()

    for copy in arrive:
        copy.wait_recv()
    wide[...] += product(from_table, table[...])
    for strip in strips:
        values = wide[strip]
        sigmoid = jax.nn.sigmoid(values)
        hidden[strip] = (values * sigmoid).astype(jnp.bfloat16)
        slope[strip] = sigmoid * (1.0 + values * (1.0 - sigmoid))

    step4(3)
    wide[...] = product(hidden[...], weights[3])
    for strip in strips:
        values = wide[strip]
        centred = values - jnp.mean(values, axis=-1, keepdims=True)
        variance = jnp.mean(centred * centred, axis=-1, keepdims=True)
        along = jnp.mean(scaled[strip] * centred, axis=-1, keepdims=True)
        scale = lax.rsqrt(variance + eps)
        unit_rows = centred * scale
        new_edge[strip] = (edge[strip].astype(jnp.float32) + unit_rows * gain[...]).astype(jnp.bfloat16)
        grad_projected[strip] = (scale * (scaled[strip] - unit_rows * (scale * along))).astype(jnp.bfloat16)

    wide[...] = rows_product(grad_projected[...], weights[3])
    for strip in strips:
        grad_preact[strip] = (wide[strip] * slope[strip]).astype(jnp.bfloat16)
    grad_table = product(to_table, grad_preact[...])
    back[...] = grad_table[count:lookup_rows].astype(jnp.bfloat16)
    home = []
    for j, shift in enumerate(shifts):
        piece = pl.ds(j * halo_rows, halo_rows)
        home.append(send(back.at[piece], returned.at[piece], at_block(-shift)))
    grad_edge[...] = (grad_total[...] + rows_product(grad_preact[...], weights[1])).astype(jnp.bfloat16)
    new_node[...] = (node[...].astype(jnp.float32) + product(to_receiver, new_edge[...])).astype(jnp.bfloat16)
    grad_nodes = node_g[...].astype(jnp.float32) + rows_product(
        grad_table[lookup_rows:].astype(jnp.bfloat16), weights[2]
    )
    for copy in home:
        copy.wait_recv()
    grad_send = (grad_table[:count] + product(pick, returned[...])).astype(jnp.bfloat16)
    grad_node[...] = (grad_nodes + rows_product(grad_send, weights[0])).astype(jnp.bfloat16)
    for copy in sent:
        copy.wait_send()


def hand_out(*refs):
    copies = [pltpu.make_async_copy(refs[i], refs[4 + i], refs[8].at[i]) for i in range(4)]
    for copy in copies:
        copy.start()
    for copy in copies:
        copy.wait()


def solution(mesh):
    doms, mps = mesh.shape["dom"], mesh.shape["mp"]

    def shards(
        node_states, edge_states, edge_weight, send_weight, receive_weight, output_weight,
        norm_gain, senders, receivers, send_rows, node_cotangent, edge_cotangent,
    ):
        nodes, width = node_states.shape
        edges = edge_states.shape[0]
        hidden = edge_weight.shape[1]
        spread, halo_rows = send_rows.shape[1] // 2, send_rows.shape[2]
        halos = 2 * spread * halo_rows
        shifts = [step + 1 for step in range(spread)] + [-(step + 1) for step in range(spread)]
        square = mps == 4 and doms % 4 == 0 and edge_weight.shape[0] % 256 == 0
        copies = (32 if square else 4 * (mps - 1)) + 4 * spread
        any_space = pl.BlockSpec(memory_space=pl.ANY)
        bf16 = jnp.bfloat16
        results = pl.pallas_call(
            functools.partial(kernel, doms, mps, square, shifts),
            out_shape=(
                pltpu.VMEM((nodes, width), bf16),
                pltpu.VMEM((edges, width), bf16),
                pltpu.VMEM((nodes, width), bf16),
                pltpu.VMEM((edges, width), bf16),
            ),
            in_specs=[pl.BlockSpec(memory_space=pltpu.HBM)] * 12,
            out_specs=(pl.BlockSpec(memory_space=pltpu.VMEM),) * 4,
            scratch_shapes=[
                pltpu.VMEM((4, width, hidden), bf16),
                pltpu.VMEM((nodes, width), bf16),
                pltpu.VMEM((edges, width), bf16),
                pltpu.VMEM((1, width), jnp.float32),
                pltpu.VMEM((1, edges), jnp.int32),
                pltpu.VMEM((1, edges), jnp.int32),
                pltpu.VMEM(send_rows.shape, jnp.int32),
                pltpu.VMEM((nodes, width), bf16),
                pltpu.VMEM((edges, width), bf16),
                pltpu.VMEM((2 * nodes + halos, hidden), bf16),
                pltpu.VMEM((halos, hidden), bf16),
                pltpu.VMEM((halos, hidden), bf16),
                pltpu.VMEM((halos, hidden), bf16),
                pltpu.VMEM((edges, hidden), jnp.float32),
                pltpu.VMEM((edges, hidden), jnp.float32),
                pltpu.VMEM((edges, width), jnp.float32),
                pltpu.VMEM((edges, width), jnp.float32),
                pltpu.VMEM((edges, hidden), bf16),
                pltpu.VMEM((edges, width), bf16),
                pltpu.VMEM((edges, hidden), bf16),
                pltpu.SemaphoreType.DMA((12,)),
                pltpu.SemaphoreType.DMA((copies,)),
                pltpu.SemaphoreType.DMA((copies,)),
            ],
            compiler_params=pltpu.CompilerParams(
                collective_id=0, has_side_effects=True, vmem_limit_bytes=60 * 1024 * 1024
            ),
            cost_estimate=pl.CostEstimate(flops=2 * width * hidden * 4 * (nodes + edges), bytes_accessed=16 * width * hidden, transcendentals=edges * hidden),
        )(
            node_states, edge_states, edge_weight, send_weight, receive_weight, output_weight,
            norm_gain.reshape(1, width), senders.reshape(1, edges), receivers.reshape(1, edges),
            send_rows, node_cotangent, edge_cotangent,
        )
        return pl.pallas_call(
            hand_out,
            out_shape=tuple(jax.ShapeDtypeStruct(result.shape, bf16) for result in results),
            in_specs=[pl.BlockSpec(memory_space=pltpu.VMEM)] * 4,
            out_specs=(any_space,) * 4,
            scratch_shapes=[pltpu.SemaphoreType.DMA((4,))],
            compiler_params=pltpu.CompilerParams(vmem_limit_bytes=8 * 1024 * 1024),
        )(*results)

    rows = P(("dom", "mp"), None)
    panel = P("mp", None)
    indices = P(("dom", "mp"))
    return jax.shard_map(
        shards,
        mesh=mesh,
        in_specs=(rows, rows, panel, panel, panel, panel, P(), indices, indices, P(("dom", "mp"), None, None), rows, rows),
        out_specs=(rows,) * 4,
        check_vma=False,
    )
```

```python
import functools

import jax
import jax.numpy as jnp
from jax import lax
from jax.experimental import pallas as pl
from jax.experimental.pallas import tpu as pltpu
from jax.sharding import PartitionSpec as P

eps = 1e-05
MESH = pl.DeviceIdType.MESH
DIAGONAL = ((0, 2, 2), (0, 2, 2), (4, 0, 0), (4, 0, 0))


def product(left, right):
    return jnp.dot(left, right, preferred_element_type=jnp.float32)


def rows_product(left, right):
    return lax.dot_general(
        left, right, (((1,), (1,)), ((), ())), preferred_element_type=jnp.float32
    )


def kernel(
    doms, mps, square, shifts,
    node_h, edge_h, edge_w, send_w, receive_w, output_w, gain_h, send_h, receive_h, rows_h, node_g_h, edge_g_h,
    new_node, new_edge, grad_node, grad_edge,
    weights, node, edge, gain, sender, receiver, rows, node_g, edge_g,
    table, halo, back, returned,
    wide, slope, grad_total, scaled, hidden, grad_projected, grad_preact,
    load_sem, send_sem, recv_sem,
):
    dom, mp = lax.axis_index("dom"), lax.axis_index("mp")
    block = dom * mps + mp
    blocks = doms * mps
    count, halo_rows = node.shape[0], halo.shape[0] // len(shifts)
    panels = (send_w, edge_w, receive_w, output_w)
    size = send_w.shape[0]

    loads = []

    def load(source, target):
        copy = pltpu.make_async_copy(source, target, load_sem.at[len(loads)])
        copy.start()
        loads.append(copy)
        return copy

    own = pl.ds(pl.multiple_of(mp * size, size), size)
    load_panel = [load(panels[w], weights.at[w, own]) for w in range(4)]
    load_node = load(node_h, node)
    load_rows = load(rows_h, rows)
    load_sender = load(send_h, sender)
    load_receiver = load(receive_h, receiver)
    load_edge = load(edge_h, edge)
    load_gain = load(gain_h, gain)
    load_node_g = load(node_g_h, node_g)
    load_edge_g = load(edge_g_h, edge_g)

    def at_block(offset):
        other = lax.rem(block + offset + blocks, blocks)
        return (lax.div(other, mps), lax.rem(other, mps))

    if square:
        x, deep = lax.rem(dom, 2), lax.rem(lax.div(dom, 2), 2)
        core, y = lax.rem(mp, 2), lax.div(mp, 2)
        twin = (dom, mp + 1 - 2 * core)
        over_y = (dom, mp + 2 - 4 * y)
        over_x = (dom + 1 - 2 * x, mp)
        over_z = (dom + 2 - 4 * deep, mp)
        peers = [twin, over_y, over_x, over_z]
    else:
        peers = [(dom, lax.rem(mp + step, mps)) for step in range(1, mps)]
    barrier = pltpu.get_barrier_semaphore()
    greeted = peers + [at_block(shift) for shift in shifts]
    for peer in greeted:
        pl.semaphore_signal(barrier, inc=1, device_id=peer, device_id_type=MESH)
    pl.semaphore_wait(barrier, len(greeted))

    sent = []

    def send(source, target, peer):
        index = len(sent)
        copy = pltpu.make_async_remote_copy(
            src_ref=source, dst_ref=target, send_sem=send_sem.at[index], recv_sem=recv_sem.at[index],
            device_id=peer, device_id_type=MESH,
        )
        copy.start()
        sent.append(copy)
        return copy

    if square:
        unit = size // 16
        quarter = size // 4
        mine = x + 2 * deep
        by_x, by_z, opposite = mine + 1 - 2 * x, mine + 2 - 4 * deep, 3 - mine
        far = (mp + 2 - 4 * y) * size
        near = mp * size

        def part(w, base, start, length):
            return weights.at[w, pl.ds(pl.multiple_of(base + start, unit), length)]

        A, B, DY, X, Z, DX, DZ, SB, SX, SZ, SD = ([None] * 4 for _ in range(11))

        def begin_twin(w):
            A[w] = send(panels[w], weights.at[w, own], twin)

        def begin(w):
            B[w] = send(
                panels[w].at[pl.ds(pl.multiple_of(mine * quarter, quarter), quarter)],
                part(w, near, mine * quarter, quarter), over_y,
            )

        def begin_diagonal(w):
            length = DIAGONAL[w][0] * unit
            DY[w] = send(
                panels[w].at[pl.ds(pl.multiple_of(opposite * quarter, quarter), length)],
                part(w, near, opposite * quarter, length), over_y,
            )

        def forward(w, start, length, peer):
            region = part(w, far, start, length)
            return send(region, region, peer)

        def step1(w):
            B[w].wait_recv()
            X[w] = forward(w, mine * quarter, quarter, over_x)
            Z[w] = forward(w, mine * quarter, quarter, over_z)
            if w == 0:
                begin(2)
            elif w == 1:
                begin(3)
            else:
                begin_diagonal(w)
            if w >= 2:
                SB[w] = forward(w, mine * quarter, quarter, twin)

        def step2(w):
            dy, dx, dz = (units * unit for units in DIAGONAL[w])
            X[w].wait_recv()
            if dz:
                DZ[w] = forward(w, by_x * quarter + dy + dx, dz, over_z)
            if w >= 2:
                SX[w] = forward(w, by_x * quarter, quarter, twin)
            Z[w].wait_recv()
            if dx:
                DX[w] = forward(w, by_z * quarter + dy, dx, over_x)
            if w >= 2:
                SZ[w] = forward(w, by_z * quarter, quarter, twin)

        def step3(w):
            for copy in (DY[w], DX[w], DZ[w]):
                if copy is not None:
                    copy.wait_recv()
            if w >= 2:
                SD[w] = forward(w, opposite * quarter, quarter, twin)
            else:
                SD[w] = forward(w, 0, size, twin)

        def step4(w):
            if w < 3:
                load_panel[w].wait()
                A[w].wait_recv()
            for copy in (SB[w], SX[w], SZ[w], SD[w]):
                if copy is not None:
                    copy.wait_recv()
    else:
        direct = [[send(panels[w], weights.at[w, own], peer) for peer in peers] for w in range(4)]

        def step4(w):
            load_panel[w].wait()
            for copy in direct[w]:
                copy.wait_recv()

    def project_send():
        load_node.wait()
        load_rows.wait()
        chosen = jnp.concatenate([rows[0, j : j + 1, :] for j in range(len(shifts))], axis=1)
        table[:count] = product(node[...], weights[0]).astype(jnp.bfloat16)
        pick = (lax.broadcasted_iota(jnp.int32, (count, halo.shape[0]), 0) == chosen).astype(jnp.float32)
        halo[...] = product(pick.T.astype(jnp.bfloat16), table[:count]).astype(jnp.bfloat16)
        arrive = []
        for j, shift in enumerate(shifts):
            arrive.append(send(
                halo.at[pl.ds(j * halo_rows, halo_rows)],
                table.at[pl.ds(count + j * halo_rows, halo_rows)], at_block(shift),
            ))
        return pick.astype(jnp.bfloat16), arrive

    lookup_rows = count + halo.shape[0]

    def project_receive():
        table[lookup_rows:] = product(node[...], weights[2]).astype(jnp.bfloat16)

    if square:
        begin(0)
        begin(1)
        begin_twin(0)
        begin_twin(1)
    for copy in (load_edge, load_sender, load_receiver, load_gain, load_node_g, load_edge_g):
        copy.wait()
    edges = edge.shape[0]
    by_sender = lax.broadcasted_iota(jnp.int32, (lookup_rows, edges), 0) == sender[...]
    by_receiver = lax.broadcasted_iota(jnp.int32, (count, edges), 0) == receiver[...]
    to_table = jnp.concatenate([by_sender.astype(jnp.float32), by_receiver.astype(jnp.float32)], axis=0)
    from_table = to_table.T.astype(jnp.bfloat16)
    to_receiver = by_receiver.astype(jnp.float32)
    from_receiver = to_receiver.T.astype(jnp.bfloat16)
    to_table = to_table.astype(jnp.bfloat16)
    to_receiver = to_receiver.astype(jnp.bfloat16)

    strips = [pl.ds(start, 16) for start in range(0, edges, 16)]
    grad_total[...] = edge_g[...].astype(jnp.float32) + product(from_receiver, node_g[...])
    for strip in strips:
        values = grad_total[strip] * gain[...]
        scaled[strip] = values - jnp.mean(values, axis=-1, keepdims=True)
    if square:
        step1(0)
        begin_twin(2)
        step1(1)
        begin_twin(3)
        step2(0)
        step1(2)
        step2(1)
        step3(0)
        step1(3)
        step2(2)
        step4(0)
        pick, arrive = project_send()
        step3(1)
        step3(2)
        step4(1)
        wide[...] = product(edge[...], weights[1])
        step2(3)
        step3(3)
        step4(2)
    else:
        step4(0)
        pick, arrive = project_send()
        step4(1)
        wide[...] = product(edge[...], weights[1])
        step4(2)
    project_receive()

    for copy in arrive:
        copy.wait_recv()
    wide[...] += product(from_table, table[...])
    for strip in strips:
        values = wide[strip]
        sigmoid = jax.nn.sigmoid(values)
        hidden[strip] = (values * sigmoid).astype(jnp.bfloat16)
        slope[strip] = sigmoid * (1.0 + values * (1.0 - sigmoid))

    if square:
        load_panel[3].wait()
        A[3].wait_recv()
        near_half = pl.ds(pl.multiple_of(y * 2 * size, 2 * size), 2 * size)
        far_half = pl.ds(pl.multiple_of((1 - y) * 2 * size, 2 * size), 2 * size)
        wide[...] = product(hidden[:, near_half], weights[3, near_half])
        step4(3)
        wide[...] += product(hidden[:, far_half], weights[3, far_half])
    else:
        step4(3)
        wide[...] = product(hidden[...], weights[3])
    for strip in strips:
        values = wide[strip]
        centred = values - jnp.mean(values, axis=-1, keepdims=True)
        variance = jnp.mean(centred * centred, axis=-1, keepdims=True)
        along = jnp.mean(scaled[strip] * centred, axis=-1, keepdims=True)
        scale = lax.rsqrt(variance + eps)
        unit_rows = centred * scale
        new_edge[strip] = (edge[strip].astype(jnp.float32) + unit_rows * gain[...]).astype(jnp.bfloat16)
        grad_projected[strip] = (scale * (scaled[strip] - unit_rows * (scale * along))).astype(jnp.bfloat16)

    wide[...] = rows_product(grad_projected[...], weights[3])
    for strip in strips:
        grad_preact[strip] = (wide[strip] * slope[strip]).astype(jnp.bfloat16)
    grad_table = product(to_table, grad_preact[...])
    back[...] = grad_table[count:lookup_rows].astype(jnp.bfloat16)
    home = []
    for j, shift in enumerate(shifts):
        piece = pl.ds(j * halo_rows, halo_rows)
        home.append(send(back.at[piece], returned.at[piece], at_block(-shift)))
    grad_edge[...] = (grad_total[...] + rows_product(grad_preact[...], weights[1])).astype(jnp.bfloat16)
    new_node[...] = (node[...].astype(jnp.float32) + product(to_receiver, new_edge[...])).astype(jnp.bfloat16)
    grad_nodes = node_g[...].astype(jnp.float32) + rows_product(
        grad_table[lookup_rows:].astype(jnp.bfloat16), weights[2]
    )
    for copy in home:
        copy.wait_recv()
    grad_send = (grad_table[:count] + product(pick, returned[...])).astype(jnp.bfloat16)
    grad_node[...] = (grad_nodes + rows_product(grad_send, weights[0])).astype(jnp.bfloat16)
    for copy in sent:
        copy.wait_send()


def hand_out(*refs):
    copies = [pltpu.make_async_copy(refs[i], refs[4 + i], refs[8].at[i]) for i in range(4)]
    for copy in copies:
        copy.start()
    for copy in copies:
        copy.wait()


def solution(mesh):
    doms, mps = mesh.shape["dom"], mesh.shape["mp"]

    def shards(
        node_states, edge_states, edge_weight, send_weight, receive_weight, output_weight,
        norm_gain, senders, receivers, send_rows, node_cotangent, edge_cotangent,
    ):
        nodes, width = node_states.shape
        edges = edge_states.shape[0]
        hidden = edge_weight.shape[1]
        spread, halo_rows = send_rows.shape[1] // 2, send_rows.shape[2]
        halos = 2 * spread * halo_rows
        shifts = [step + 1 for step in range(spread)] + [-(step + 1) for step in range(spread)]
        square = mps == 4 and doms % 4 == 0 and edge_weight.shape[0] % 256 == 0
        copies = (32 if square else 4 * (mps - 1)) + 4 * spread
        any_space = pl.BlockSpec(memory_space=pl.ANY)
        bf16 = jnp.bfloat16
        results = pl.pallas_call(
            functools.partial(kernel, doms, mps, square, shifts),
            out_shape=(
                pltpu.VMEM((nodes, width), bf16),
                pltpu.VMEM((edges, width), bf16),
                pltpu.VMEM((nodes, width), bf16),
                pltpu.VMEM((edges, width), bf16),
            ),
            in_specs=[pl.BlockSpec(memory_space=pltpu.HBM)] * 12,
            out_specs=(pl.BlockSpec(memory_space=pltpu.VMEM),) * 4,
            scratch_shapes=[
                pltpu.VMEM((4, width, hidden), bf16),
                pltpu.VMEM((nodes, width), bf16),
                pltpu.VMEM((edges, width), bf16),
                pltpu.VMEM((1, width), jnp.float32),
                pltpu.VMEM((1, edges), jnp.int32),
                pltpu.VMEM((1, edges), jnp.int32),
                pltpu.VMEM(send_rows.shape, jnp.int32),
                pltpu.VMEM((nodes, width), bf16),
                pltpu.VMEM((edges, width), bf16),
                pltpu.VMEM((2 * nodes + halos, hidden), bf16),
                pltpu.VMEM((halos, hidden), bf16),
                pltpu.VMEM((halos, hidden), bf16),
                pltpu.VMEM((halos, hidden), bf16),
                pltpu.VMEM((edges, hidden), jnp.float32),
                pltpu.VMEM((edges, hidden), jnp.float32),
                pltpu.VMEM((edges, width), jnp.float32),
                pltpu.VMEM((edges, width), jnp.float32),
                pltpu.VMEM((edges, hidden), bf16),
                pltpu.VMEM((edges, width), bf16),
                pltpu.VMEM((edges, hidden), bf16),
                pltpu.SemaphoreType.DMA((12,)),
                pltpu.SemaphoreType.DMA((copies,)),
                pltpu.SemaphoreType.DMA((copies,)),
            ],
            compiler_params=pltpu.CompilerParams(
                collective_id=0, has_side_effects=True, vmem_limit_bytes=60 * 1024 * 1024
            ),
            cost_estimate=pl.CostEstimate(flops=2 * width * hidden * 4 * (nodes + edges), bytes_accessed=16 * width * hidden, transcendentals=edges * hidden),
        )(
            node_states, edge_states, edge_weight, send_weight, receive_weight, output_weight,
            norm_gain.reshape(1, width), senders.reshape(1, edges), receivers.reshape(1, edges),
            send_rows, node_cotangent, edge_cotangent,
        )
        return pl.pallas_call(
            hand_out,
            out_shape=tuple(jax.ShapeDtypeStruct(result.shape, bf16) for result in results),
            in_specs=[pl.BlockSpec(memory_space=pltpu.VMEM)] * 4,
            out_specs=(any_space,) * 4,
            scratch_shapes=[pltpu.SemaphoreType.DMA((4,))],
            compiler_params=pltpu.CompilerParams(vmem_limit_bytes=8 * 1024 * 1024),
        )(*results)

    rows = P(("dom", "mp"), None)
    panel = P("mp", None)
    indices = P(("dom", "mp"))
    return jax.shard_map(
        shards,
        mesh=mesh,
        in_specs=(rows, rows, panel, panel, panel, panel, P(), indices, indices, P(("dom", "mp"), None, None), rows, rows),
        out_specs=(rows,) * 4,
        check_vma=False,
    )
```
